256 devices in a mesh: seq: 32 (over y, x, core), head: 8 (over z).
Axes of the slice: x: 4, y: 4, z: 8, core: 2. Of those that a mesh axis runs over, the one named last changes fastest.
Arguments:
- tokens: bfloat16 [16384, 6144], P('seq', 'head'), may hold values from -6 to 6
- w_query: bfloat16 [6144, 4096], P('seq', 'head'), may hold values from -0.078125 to 0.078125
- w_key: bfloat16 [6144, 4096], P('seq', 'head'), may hold values from -0.078125 to 0.078125
- w_value: bfloat16 [6144, 4096], P('seq', 'head'), may hold values from -0.078125 to 0.078125
- gain: float32 [4096], P('head'), may hold values from 0.1 to 1.9
Outputs:
- output: bfloat16 [16384, 4096], P('seq', 'head')
The draws below stay inside these ranges and needn't reach their ends.
All inputs are finite; a program needn't handle non-finite values.
Results may differ from the reference program's by a relative error of at most 0.007.
Values may be sent and summed in bfloat16 or wider, within the bound.
No kernel may reach another device: no remote copies, remote signals or barrier semaphores. Data moves between devices by JAX's collectives and lax.ppermute only.
A program may use at most 128 MiB of HBM per device.

```python
import jax
import jax.numpy as jnp
from jax import lax

D = 6144
HEADS = 32
HDIM = 128
SPAN = 256
HD = 4096
TOKENS = 16384


def block_levels(rng, extent, pieces, low, high):
    def one(axis_at, blocks):
        draws = jax.random.uniform(jax.random.fold_in(jax.random.fold_in(rng, 6), axis_at), (blocks,), jnp.float32, low / len(pieces), high / len(pieces))
        return jnp.repeat(jnp.exp(draws), extent[axis_at] // blocks).reshape((-1,) + (1,) * (len(extent) - axis_at - 1))

    factor_of = one(*pieces[0])
    for cut in pieces[1:]:
        factor_of = factor_of * one(*cut)
    return factor_of


def scatter_about(rng, shape, spread, most, shards=(), dtype=jnp.bfloat16):
    drawn = spread * jax.random.normal(rng, shape, jnp.float32)
    if shards:
        drawn = drawn * block_levels(rng, shape, shards, -0.22, 0.18)
    return jnp.clip(drawn, -most, most).astype(dtype)


def setup_inputs(seed: int = 0) -> dict:
    key_list = jax.random.split(jax.random.key(seed), 6)
    tokens = scatter_about(key_list[0], (TOKENS, D), 1.0, 6.0, ((0, 32), (1, 8)))
    w_query = scatter_about(key_list[1], (D, HD), D ** -0.5, 0.078125, ((0, 32), (1, 8)))
    w_key = scatter_about(key_list[2], (D, HD), D ** -0.5, 0.078125, ((0, 32), (1, 8)))
    w_value = scatter_about(key_list[3], (D, HD), D ** -0.5, 0.078125, ((0, 32), (1, 8)))
    gain = jnp.clip(1.0 + 0.18 * jax.random.normal(key_list[4], (HD,), jnp.float32), 0.1, 1.9)
    return dict(tokens=tokens, w_query=w_query, w_key=w_key, w_value=w_value, gain=gain)


def reference(tokens, w_query, w_key, w_value, gain):

    def project(weight):
        return jax.nn.silu(jnp.dot(tokens, weight, preferred_element_type=jnp.float32)).astype(jnp.bfloat16)
    blocks = TOKENS // SPAN
    query_blocks = project(w_query).reshape(blocks, SPAN, HEADS, HDIM).astype(jnp.float32)
    key_blocks = project(w_key).reshape(blocks, SPAN, HEADS, HDIM).astype(jnp.float32)
    value_blocks = project(w_value).reshape(blocks, SPAN, HEADS, HDIM).astype(jnp.float32)
    highest = lax.Precision.HIGHEST
    pair_states = jnp.einsum('cshd,cshe->chde', key_blocks, value_blocks, precision=highest)
    prefix = jnp.cumsum(pair_states, axis=0) - pair_states
    states = prefix.astype(jnp.bfloat16).astype(jnp.float32)
    scores = jnp.einsum('cshd,cthd->chst', query_blocks, key_blocks, precision=highest)
    causal = jnp.arange(SPAN)[:, None] >= jnp.arange(SPAN)[None, :]
    scores = jnp.where(causal[None, None], scores, 0.0).astype(jnp.bfloat16).astype(jnp.float32)
    local_part = jnp.einsum('chst,cthe->cshe', scores, value_blocks, precision=highest)
    carried = jnp.einsum('cshd,chde->cshe', query_blocks, states, precision=highest)
    attended = local_part + carried
    inverse_rms = lax.rsqrt(lax.optimization_barrier(jnp.mean(attended * attended, axis=-1, keepdims=True)) + 1e-06)
    return (attended * inverse_rms * gain.reshape(HEADS, HDIM)).astype(jnp.bfloat16).reshape(TOKENS, HD)
```

```python
import jax
import jax.numpy as jnp
from jax import lax
from jax.sharding import PartitionSpec as P

HDIM = 128
SPAN = 256
X, Y, C = 4, 4, 2


def seq_of(y, x, c):
    return (y * X + x) * C + c


def shift_x(k):
    return [
        (seq_of(y, x, c), seq_of(y, x + k, c))
        for y in range(Y)
        for x in range(X)
        for c in range(C)
        if 0 <= x + k < X
    ]


def spin_x(k):
    return [
        (seq_of(y, x, c), seq_of(y, (x + k) % X, c))
        for y in range(Y)
        for x in range(X)
        for c in range(C)
    ]


def shift_y(k):
    return [
        (seq_of(y, x, c), seq_of(y + k, x, c))
        for y in range(Y)
        for x in range(X)
        for c in range(C)
        if 0 <= y + k < Y
    ]


def swap_core():
    return [(s, s ^ 1) for s in range(X * Y * C)]


def earlier_slabs(total):
    me = lax.axis_index("seq")
    core = me % C
    x = (me // C) % X
    other = lax.ppermute(total.astype(jnp.bfloat16), "seq", swap_core()).astype(jnp.float32)
    before = jnp.where(core == 1, other, 0.0)
    chip = (total + other).astype(jnp.bfloat16)
    row = chip.astype(jnp.float32)
    for k in range(1, X):
        got = lax.ppermute(chip, "seq", spin_x(k)).astype(jnp.float32)
        row = row + got
        before = before + jnp.where(x >= k, got, 0.0)
    row = row.astype(jnp.bfloat16)
    for k in range(1, Y):
        before = before + lax.ppermute(row, "seq", shift_y(k)).astype(jnp.float32)
    return before


def gather_tokens(tokens):
    n = lax.axis_size("head")
    z = lax.axis_index("head")
    rows, depth = tokens.shape
    up = [(i, (i + 1) % n) for i in range(n)]
    down = [(i, (i - 1) % n) for i in range(n)]
    whole = jnp.zeros((rows, n * depth), tokens.dtype)

    def put(whole, piece, at, row=0):
        return lax.dynamic_update_slice(whole, piece, (row, (at % n) * depth))

    whole = put(whole, tokens, z)
    a = b = tokens
    for step in range(1, n // 2):
        a = lax.ppermute(a, "head", up)
        b = lax.ppermute(b, "head", down)
        whole = put(whole, a, z - step + n)
        whole = put(whole, b, z + step)
    half = rows // 2
    a = lax.ppermute(a[:half], "head", up)
    b = lax.ppermute(b[half:], "head", down)
    whole = put(whole, a, z + n // 2)
    whole = put(whole, b, z + n // 2, half)
    return whole


def local(tokens, w_query, w_key, w_value, gain):
    weights = lax.all_gather(
        jnp.concatenate([w_key, w_value, w_query], axis=1), "seq", axis=0, tiled=True
    )
    whole = gather_tokens(tokens)
    tok_rows = whole.shape[0]
    columns_here = w_query.shape[1]
    heads_here = columns_here // HDIM
    blocks = tok_rows // SPAN

    def project(low, high):
        return jax.nn.silu(
            jnp.dot(whole, weights[:, low:high], preferred_element_type=jnp.float32)
        ).astype(jnp.bfloat16)

    def to_blocks(values):
        return values.reshape(blocks, SPAN, heads_here, HDIM)

    key_value = project(0, 2 * columns_here)
    key_blocks = to_blocks(key_value[:, :columns_here])
    value_blocks = to_blocks(key_value[:, columns_here:])
    query_blocks = to_blocks(project(2 * columns_here, 3 * columns_here))
    pair_states = jnp.einsum(
        "cshd,cshe->chde", key_blocks, value_blocks, preferred_element_type=jnp.float32
    )
    slab_total = jnp.sum(pair_states, axis=0)
    within = jnp.cumsum(pair_states, axis=0) - pair_states
    earlier = earlier_slabs(slab_total)
    states = (earlier[None] + within).astype(jnp.bfloat16)
    scores = jnp.einsum(
        "cshd,cthd->chst", query_blocks, key_blocks, preferred_element_type=jnp.float32
    )
    causal = lax.broadcasted_iota(jnp.int32, (SPAN, SPAN), 0) >= lax.broadcasted_iota(
        jnp.int32, (SPAN, SPAN), 1
    )
    scores = jnp.where(causal[None, None], scores, 0.0).astype(jnp.bfloat16)
    local_part = jnp.einsum(
        "chst,cthe->cshe", scores, value_blocks, preferred_element_type=jnp.float32
    )
    carried = jnp.einsum(
        "cshd,chde->cshe", query_blocks, states, preferred_element_type=jnp.float32
    )
    attended = local_part + carried
    inverse_rms = lax.rsqrt(jnp.mean(attended * attended, axis=-1, keepdims=True) + 1e-06)
    return (
        (attended * inverse_rms * gain.reshape(heads_here, HDIM))
        .astype(jnp.bfloat16)
        .reshape(tok_rows, columns_here)
    )


def solution(mesh):
    in_specs = (P("seq", "head"), P("seq", "head"), P("seq", "head"), P("seq", "head"), P("head"))
    out_specs = P("seq", "head")
    return jax.shard_map(local, mesh=mesh, in_specs=in_specs, out_specs=out_specs, check_vma=False)
```

```python
import functools

import jax
import jax.numpy as jnp
import numpy as np
from jax import lax
from jax.experimental import pallas as pl
from jax.experimental.pallas import tpu as pltpu
from jax.sharding import PartitionSpec as P

HDIM = 128
SPAN = 256
Y, X, C, Z = 4, 4, 2, 8
ROWS = 192
PIECE = 2 * ROWS
SLAB = 512
CHIP = C * SLAB
HALF = 256
F32, BF16 = jnp.float32, jnp.bfloat16
DIMS = (
    lambda y, x: (y, x ^ 1),
    lambda y, x: (y ^ 1, x),
    lambda y, x: (y, x ^ 3),
    lambda y, x: (y ^ 3, x),
)
ANY = pl.BlockSpec(memory_space=pl.ANY)
VMEM = pl.BlockSpec(memory_space=pltpu.VMEM)
SMEM = pl.BlockSpec(memory_space=pltpu.SMEM)


def seq_of(y, x, c):
    return (y * X + x) * C + c


def chips():
    return [(y, x) for y in range(Y) for x in range(X)]


def dim_of(stream, core, step):
    return (2 * stream + core + step) % 4


def cube_pairs(stream, step):
    return [
        (seq_of(y, x, c), seq_of(*DIMS[dim_of(stream, c, step)](y, x), c))
        for y, x in chips()
        for c in range(C)
    ]


def ring_pairs():
    return [
        (s * Z + z, s * Z + (z + (1 if s % C == 0 else -1)) % Z)
        for s in range(Y * X * C)
        for z in range(Z)
    ]


SWAP = [(s, s ^ 1) for s in range(Y * X * C)]


def spin_x(k):
    return [(seq_of(y, x, c), seq_of(y, (x + k) % X, c)) for y, x in chips() for c in range(C)]


def shift_y(k):
    return [
        (seq_of(y, x, c), seq_of(y + k, x, c)) for y, x in chips() for c in range(C) if y + k < Y
    ]


def place_table():
    table = np.zeros((Y * X * C, Z, 2, Z, 2), np.int32)
    for y, x in chips():
        for c in range(C):
            for z in range(Z):
                for stream in range(2):
                    for k in range(Z):
                        for e in range(2):
                            source = 2 * ((z - k if c == 0 else z + k) % Z) + e
                            dx, dy = (source % X) ^ x, (source // X) ^ y
                            bits = (
                                (dx & 1) ^ (dx >> 1),
                                (dy & 1) ^ (dy >> 1),
                                dx >> 1,
                                dy >> 1,
                            )
                            table[seq_of(y, x, c), z, stream, k, e] = sum(
                                bits[dim_of(stream, c, step)] << step for step in range(4)
                            )
    return table.reshape(Y * X * C * Z, 4 * Z)


def silu(u):
    return u / (1.0 + jnp.exp(-u))


def product_kernel(parts, info, *refs):
    tokens, refs = refs[: 2 * Z], refs[2 * Z :]
    weights, refs = refs[:4], refs[4:]
    outs, refs = refs[: len(parts)], refs[len(parts) :]
    whole, piled, total, token_sem, weight_sem = refs
    core = info[0]
    groups = 2
    per = Z // groups
    depth = per * PIECE

    def weight_copy(source, part, at, columns, row):
        return pltpu.make_async_copy(
            source.at[pl.ds(pl.multiple_of(row * ROWS, ROWS), ROWS), columns],
            piled.at[part, pl.ds(at * ROWS, ROWS)],
            weight_sem.at[part, at],
        )

    for k in range(Z):
        for slab in range(2):
            first = pl.multiple_of(SLAB * (core if slab == 0 else 1 - core), SLAB)
            pltpu.make_async_copy(
                tokens[2 * k + slab],
                whole.at[pl.ds(first, SLAB), pl.ds(k * PIECE, PIECE)],
                token_sem.at[k, slab],
            ).start()
        for part, (mine, low, high) in enumerate(parts):
            half = core if mine else 1 - core
            for e in range(2):
                place = info[1 + half * 2 * Z + 2 * k + e]
                choice = half * 2 + place // 8
                for b in range(4):

                    @pl.when(choice == b)
                    def _():
                        weight_copy(
                            weights[b], part, 2 * k + e, pl.ds(low, high - low), place % 8
                        ).start()

    for g in range(groups):
        for k in range(g * per, (g + 1) * per):
            for slab in range(2):
                pltpu.make_async_copy(
                    tokens[2 * k + slab],
                    whole.at[pl.ds(0, SLAB), pl.ds(k * PIECE, PIECE)],
                    token_sem.at[k, slab],
                ).wait()
            for part, (mine, low, high) in enumerate(parts):
                for e in range(2):
                    weight_copy(weights[0], part, 2 * k + e, pl.ds(low, high - low), 0).wait()
        for part in range(len(parts)):
            for n in range(0, outs[part].shape[1], 256):

                @pl.loop(0, CHIP // 512)
                def _(m):
                    rows = pl.ds(pl.multiple_of(m * 512, 512), 512)
                    some = jnp.dot(
                        whole[rows, g * depth : (g + 1) * depth],
                        piled[part, g * depth : (g + 1) * depth, n : n + 256],
                        preferred_element_type=F32,
                    )
                    if g == 0:
                        total[part, rows, n : n + 256] = some
                    else:
                        outs[part][rows, n : n + 256] = (
                            total[part, rows, n : n + 256] + some
                        ).astype(outs[part].dtype)


def product(info, tokens, weights, parts):
    wide = max(high - low for _, low, high in parts)
    flops = sum(2 * CHIP * Z * PIECE * (high - low) for _, low, high in parts)
    return pl.pallas_call(
        functools.partial(product_kernel, parts),
        out_shape=[
            jax.ShapeDtypeStruct((CHIP, high - low), F32 if mine else BF16)
            for mine, low, high in parts
        ],
        in_specs=[SMEM] + [ANY] * (2 * Z + 4),
        out_specs=[VMEM] * len(parts),
        scratch_shapes=[
            pltpu.VMEM((CHIP, Z * PIECE), BF16),
            pltpu.VMEM((len(parts), Z * PIECE, wide), BF16),
            pltpu.VMEM((len(parts), CHIP, wide), F32),
            pltpu.SemaphoreType.DMA((Z, 2)),
            pltpu.SemaphoreType.DMA((len(parts), 2 * Z)),
        ],
        compiler_params=pltpu.CompilerParams(vmem_limit_bytes=40 * 2**20),
        cost_estimate=pl.CostEstimate(
            flops=flops, bytes_accessed=16 * 2**20, transcendentals=0
        ),
    )(info, *tokens, *weights)


def pairs_kernel(mine, other, key, value, within, total):
    for h in range(2):
        running = jnp.zeros((HDIM, HDIM), F32)
        for b in range(CHIP // SPAN):
            rows = slice(b * SPAN, (b + 1) * SPAN)
            got = []
            for at, out in ((0, key), (HALF, value)):
                cols = slice(at + h * HDIM, at + (h + 1) * HDIM)
                u = mine[rows, cols] + other[rows, cols].astype(F32)
                got.append(silu(u).astype(BF16))
                out[rows, h * HDIM : (h + 1) * HDIM] = got[-1]
            within[b, h] = running
            running = running + lax.dot_general(
                *got, (((0,), (0,)), ((), ())), preferred_element_type=F32
            )
        total[h] = running.astype(BF16)


def pair_states(mine, other):
    return pl.pallas_call(
        pairs_kernel,
        out_shape=[
            jax.ShapeDtypeStruct((CHIP, HALF), BF16),
            jax.ShapeDtypeStruct((CHIP, HALF), BF16),
            jax.ShapeDtypeStruct((CHIP // SPAN, 2, HDIM, HDIM), F32),
            jax.ShapeDtypeStruct((2, HDIM, HDIM), BF16),
        ],
        in_specs=[VMEM] * 2,
        out_specs=[VMEM] * 4,
        compiler_params=pltpu.CompilerParams(vmem_limit_bytes=32 * 2**20),
        cost_estimate=pl.CostEstimate(
            flops=2 * CHIP * 2 * HDIM * HDIM, bytes_accessed=5 * 2**20, transcendentals=CHIP * 512
        ),
    )(mine, other)


def local_kernel(mine, other, key, value, query, inside):
    causal = lax.broadcasted_iota(jnp.int32, (SPAN, SPAN), 0) >= lax.broadcasted_iota(
        jnp.int32, (SPAN, SPAN), 1
    )
    for b in range(CHIP // SPAN):
        for h in range(2):
            at = (slice(b * SPAN, (b + 1) * SPAN), slice(h * HDIM, (h + 1) * HDIM))
            q = silu(mine[at] + other[at].astype(F32)).astype(BF16)
            query[at] = q
            scores = lax.dot_general(
                q, key[at], (((1,), (1,)), ((), ())), preferred_element_type=F32
            )
            scores = jnp.where(causal, scores, 0.0).astype(BF16)
            inside[at] = jnp.dot(scores, value[at], preferred_element_type=F32)


def local_part(mine, other, key, value):
    return pl.pallas_call(
        local_kernel,
        out_shape=[
            jax.ShapeDtypeStruct((CHIP, HALF), BF16),
            jax.ShapeDtypeStruct((CHIP, HALF), F32),
        ],
        in_specs=[VMEM] * 4,
        out_specs=[VMEM] * 2,
        compiler_params=pltpu.CompilerParams(vmem_limit_bytes=32 * 2**20),
        cost_estimate=pl.CostEstimate(
            flops=8 * CHIP * SPAN * HDIM, bytes_accessed=5 * 2**20, transcendentals=CHIP * HALF
        ),
    )(mine, other, key, value)


def finish_kernel(mine, info, query, inside, within, before, rows_0, rows_1, rows_2, gain, out):
    core = info[0]
    first = core if mine else 1 - core
    for h in range(2):
        cols = slice(h * HDIM, (h + 1) * HDIM)
        earlier = before[h]
        for rows in (rows_0, rows_1, rows_2):
            earlier = earlier + rows[h].astype(F32)
        for b in range(SLAB // SPAN):
            at = pl.ds(pl.multiple_of(first * SLAB + b * SPAN, SPAN), SPAN)
            state = (earlier + within[first * (SLAB // SPAN) + b, h]).astype(BF16)
            attended = inside[at, cols] + jnp.dot(
                query[at, cols], state, preferred_element_type=F32
            )
            scale = lax.rsqrt(jnp.mean(attended * attended, axis=-1, keepdims=True) + 1e-06)
            out[b * SPAN : (b + 1) * SPAN, cols] = (attended * scale * gain[:, cols]).astype(BF16)


def finish(mine, *args):
    return pl.pallas_call(
        functools.partial(finish_kernel, mine),
        out_shape=jax.ShapeDtypeStruct((SLAB, HALF), BF16),
        in_specs=[SMEM] + [VMEM] * 8,
        out_specs=VMEM,
        compiler_params=pltpu.CompilerParams(vmem_limit_bytes=32 * 2**20),
        cost_estimate=pl.CostEstimate(
            flops=4 * SLAB * HDIM * HDIM, bytes_accessed=2 * 2**20, transcendentals=0
        ),
    )(*args)


def after(value, *others):
    return lax.optimization_barrier((value, others))[0]


def gather(tokens, weights, core):
    even = jnp.concatenate([tokens[:, :ROWS], tokens[:, 2 * ROWS : 3 * ROWS]], axis=1)
    odd = jnp.concatenate([tokens[:, ROWS : 2 * ROWS], tokens[:, 3 * ROWS :]], axis=1)
    own = jnp.where(core == 0, even, odd)
    theirs = lax.ppermute(jnp.where(core == 0, odd, even), "seq", SWAP)
    ring = ring_pairs()
    pieces = [[own, theirs]]
    for _ in range(1, Z):
        pieces.append([lax.ppermute(p, ("seq", "head"), ring) for p in pieces[-1]])
    gates = (None, (1, 0), (2, 1), (4, 0))
    streams = list(weights)
    blocks = []
    for step in range(4):
        for j in range(2):
            if gates[step] is not None:
                k, slab = gates[step]
                streams[j] = after(streams[j], pieces[k][slab])
            got = lax.ppermute(streams[j], "seq", cube_pairs(j, step))
            if step < 3:
                streams[j] = jnp.concatenate([streams[j], got], axis=0)
            else:
                blocks += [streams[j], got]
    return [p for pair in pieces for p in pair], blocks


def local(tokens, w_query, w_key, w_value, gain):
    seq = lax.axis_index("seq")
    core = seq % C
    x = (seq // C) % X
    info = jnp.concatenate(
        [
            core[None].astype(jnp.int32),
            jnp.asarray(place_table())[seq * Z + lax.axis_index("head")],
        ]
    )
    halves = [
        jnp.concatenate([w[:, j * HALF : (j + 1) * HALF] for w in (w_key, w_value, w_query)], axis=1)
        for j in range(2)
    ]
    pieces, blocks = gather(tokens, halves, core)

    (kv_theirs,) = product(info, pieces, blocks, ((False, 0, 2 * HALF),))
    kv_got = lax.ppermute(kv_theirs, "seq", SWAP)
    (kv_mine,) = product(info, pieces, blocks, ((True, 0, 2 * HALF),))
    key, value, within, total = pair_states(kv_mine, kv_got)

    row = total.astype(F32)
    before = jnp.zeros_like(row)
    for k in range(1, X):
        got = lax.ppermute(total, "seq", spin_x(k)).astype(F32)
        row = row + got
        before = before + jnp.where(x >= k, got, 0.0)
    row = row.astype(BF16)
    rows = [lax.ppermute(row, "seq", shift_y(k)) for k in range(1, Y)]

    q_theirs, q_mine = product(
        info, pieces, blocks, ((False, 2 * HALF, 3 * HALF), (True, 2 * HALF, 3 * HALF))
    )
    q_got = lax.ppermute(q_theirs, "seq", SWAP)
    query, inside = local_part(q_mine, q_got, key, value)

    gain_here = lax.dynamic_slice(gain, (core * HALF,), (HALF,)).reshape(1, HALF)
    last = (info, query, inside, within, before, *rows, gain_here)
    out_got = lax.ppermute(finish(False, *last), "seq", SWAP)
    out_mine = finish(True, *last)
    return jnp.concatenate(
        [jnp.where(core == 0, out_mine, out_got), jnp.where(core == 0, out_got, out_mine)], axis=1
    )


def solution(mesh):
    in_specs = (P("seq", "head"), P("seq", "head"), P("seq", "head"), P("seq", "head"), P("head"))
    out_specs = P("seq", "head")
    return jax.shard_map(local, mesh=mesh, in_specs=in_specs, out_specs=out_specs, check_vma=False)
```

```python
import functools

import jax
import jax.numpy as jnp
import numpy as np
from jax import lax
from jax.experimental import pallas as pl
from jax.experimental.pallas import tpu as pltpu
from jax.sharding import PartitionSpec as P

HDIM = 128
SPAN = 256
Y, X, C, Z = 4, 4, 2, 8
ROWS = 192
PIECE = 2 * ROWS
SLAB = 512
CHIP = C * SLAB
HALF = 256
F32, BF16 = jnp.float32, jnp.bfloat16
DIMS = (
    lambda y, x: (y, x ^ 1),
    lambda y, x: (y ^ 1, x),
    lambda y, x: (y, x ^ 3),
    lambda y, x: (y ^ 3, x),
)
ANY = pl.BlockSpec(memory_space=pl.ANY)
VMEM = pl.BlockSpec(memory_space=pltpu.VMEM)
SMEM = pl.BlockSpec(memory_space=pltpu.SMEM)


def seq_of(y, x, c):
    return (y * X + x) * C + c


def chips():
    return [(y, x) for y in range(Y) for x in range(X)]


def dim_of(stream, core, step):
    return (2 * stream + core + step) % 4


def cube_pairs(stream, step):
    return [
        (seq_of(y, x, c), seq_of(*DIMS[dim_of(stream, c, step)](y, x), c))
        for y, x in chips()
        for c in range(C)
    ]


def ring_pairs():
    return [
        (s * Z + z, s * Z + (z + (1 if s % C == 0 else -1)) % Z)
        for s in range(Y * X * C)
        for z in range(Z)
    ]


SWAP = [(s, s ^ 1) for s in range(Y * X * C)]


def spin_x(k):
    return [(seq_of(y, x, c), seq_of(y, (x + k) % X, c)) for y, x in chips() for c in range(C)]


def shift_y(k):
    return [
        (seq_of(y, x, c), seq_of(y + k, x, c)) for y, x in chips() for c in range(C) if y + k < Y
    ]


def place_table():
    table = np.zeros((Y * X * C, Z, 2, Z, 2), np.int32)
    for y, x in chips():
        for c in range(C):
            for z in range(Z):
                for stream in range(2):
                    for k in range(Z):
                        for e in range(2):
                            source = 2 * ((z - k if c == 0 else z + k) % Z) + e
                            dx, dy = (source % X) ^ x, (source // X) ^ y
                            bits = (
                                (dx & 1) ^ (dx >> 1),
                                (dy & 1) ^ (dy >> 1),
                                dx >> 1,
                                dy >> 1,
                            )
                            table[seq_of(y, x, c), z, stream, k, e] = sum(
                                bits[dim_of(stream, c, step)] << step for step in range(4)
                            )
    return table.reshape(Y * X * C * Z, 4 * Z)


def silu(u):
    return u / (1.0 + jnp.exp(-u))


def product_kernel(parts, info, *refs):
    tokens, refs = refs[: 2 * Z], refs[2 * Z :]
    weights, refs = refs[:4], refs[4:]
    outs, (piled,) = refs[: len(parts)], refs[len(parts) :]
    core = info[0]
    deep = 2 * PIECE
    for part, (mine, low, high) in enumerate(parts):
        half = core if mine else 1 - core
        for at in range(2 * Z):
            place = info[1 + half * 2 * Z + at]
            row = pl.ds(pl.multiple_of((place % 8) * ROWS, ROWS), ROWS)
            choice = half * 2 + place // 8
            for b in range(4):

                @pl.when(choice == b)
                def _():
                    piled[at * ROWS : (at + 1) * ROWS, 0 : high - low] = weights[b][row, low:high]

        for slab in range(2):
            first = pl.multiple_of(SLAB * (core if slab == 0 else 1 - core), SLAB)
            for n in range(0, high - low, 256):
                total = None
                for k in range(0, Z, 2):
                    piece = jnp.concatenate(
                        [tokens[2 * k + slab][...], tokens[2 * k + 2 + slab][...]], axis=1
                    )
                    some = jnp.dot(
                        piece,
                        piled[k * PIECE : k * PIECE + deep, n : n + 256],
                        preferred_element_type=F32,
                    )
                    total = some if total is None else total + some
                outs[part][pl.ds(first, SLAB), n : n + 256] = total.astype(outs[part].dtype)


def product(info, tokens, weights, parts):
    wide = max(high - low for _, low, high in parts)
    flops = sum(2 * CHIP * Z * PIECE * (high - low) for _, low, high in parts)
    return pl.pallas_call(
        functools.partial(product_kernel, parts),
        out_shape=[
            jax.ShapeDtypeStruct((CHIP, high - low), F32 if mine else BF16)
            for mine, low, high in parts
        ],
        in_specs=[SMEM] + [VMEM] * (2 * Z + 4),
        out_specs=[VMEM] * len(parts),
        scratch_shapes=[pltpu.VMEM((Z * PIECE, wide), BF16)],
        compiler_params=pltpu.CompilerParams(vmem_limit_bytes=20 * 2**20),
        cost_estimate=pl.CostEstimate(
            flops=flops, bytes_accessed=16 * 2**20, transcendentals=0
        ),
    )(info, *tokens, *weights)


def pairs_kernel(mine, other, key, value, within, total):
    for h in range(2):
        running = jnp.zeros((HDIM, HDIM), F32)
        for b in range(CHIP // SPAN):
            rows = slice(b * SPAN, (b + 1) * SPAN)
            got = []
            for at, out in ((0, key), (HALF, value)):
                cols = slice(at + h * HDIM, at + (h + 1) * HDIM)
                u = mine[rows, cols] + other[rows, cols].astype(F32)
                got.append(silu(u).astype(BF16))
                out[rows, h * HDIM : (h + 1) * HDIM] = got[-1]
            within[b, h] = running
            running = running + lax.dot_general(
                *got, (((0,), (0,)), ((), ())), preferred_element_type=F32
            )
        total[h] = running.astype(BF16)


def pair_states(mine, other):
    return pl.pallas_call(
        pairs_kernel,
        out_shape=[
            jax.ShapeDtypeStruct((CHIP, HALF), BF16),
            jax.ShapeDtypeStruct((CHIP, HALF), BF16),
            jax.ShapeDtypeStruct((CHIP // SPAN, 2, HDIM, HDIM), F32),
            jax.ShapeDtypeStruct((2, HDIM, HDIM), BF16),
        ],
        in_specs=[VMEM] * 2,
        out_specs=[VMEM] * 4,
        compiler_params=pltpu.CompilerParams(vmem_limit_bytes=32 * 2**20),
        cost_estimate=pl.CostEstimate(
            flops=2 * CHIP * 2 * HDIM * HDIM, bytes_accessed=5 * 2**20, transcendentals=CHIP * 512
        ),
    )(mine, other)


def local_kernel(mine, other, key, value, query, inside):
    causal = lax.broadcasted_iota(jnp.int32, (SPAN, SPAN), 0) >= lax.broadcasted_iota(
        jnp.int32, (SPAN, SPAN), 1
    )
    for b in range(CHIP // SPAN):
        for h in range(2):
            at = (slice(b * SPAN, (b + 1) * SPAN), slice(h * HDIM, (h + 1) * HDIM))
            q = silu(mine[at] + other[at].astype(F32)).astype(BF16)
            query[at] = q
            scores = lax.dot_general(
                q, key[at], (((1,), (1,)), ((), ())), preferred_element_type=F32
            )
            scores = jnp.where(causal, scores, 0.0).astype(BF16)
            inside[at] = jnp.dot(scores, value[at], preferred_element_type=F32)


def local_part(mine, other, key, value):
    return pl.pallas_call(
        local_kernel,
        out_shape=[
            jax.ShapeDtypeStruct((CHIP, HALF), BF16),
            jax.ShapeDtypeStruct((CHIP, HALF), F32),
        ],
        in_specs=[VMEM] * 4,
        out_specs=[VMEM] * 2,
        compiler_params=pltpu.CompilerParams(vmem_limit_bytes=32 * 2**20),
        cost_estimate=pl.CostEstimate(
            flops=8 * CHIP * SPAN * HDIM, bytes_accessed=5 * 2**20, transcendentals=CHIP * HALF
        ),
    )(mine, other, key, value)


def finish_kernel(mine, info, query, inside, within, before, rows_0, rows_1, rows_2, gain, out):
    core = info[0]
    first = core if mine else 1 - core
    for h in range(2):
        cols = slice(h * HDIM, (h + 1) * HDIM)
        earlier = before[h]
        for rows in (rows_0, rows_1, rows_2):
            earlier = earlier + rows[h].astype(F32)
        for b in range(SLAB // SPAN):
            at = pl.ds(pl.multiple_of(first * SLAB + b * SPAN, SPAN), SPAN)
            state = (earlier + within[first * (SLAB // SPAN) + b, h]).astype(BF16)
            attended = inside[at, cols] + jnp.dot(
                query[at, cols], state, preferred_element_type=F32
            )
            scale = lax.rsqrt(jnp.mean(attended * attended, axis=-1, keepdims=True) + 1e-06)
            out[b * SPAN : (b + 1) * SPAN, cols] = (attended * scale * gain[:, cols]).astype(BF16)


def finish(mine, *args):
    return pl.pallas_call(
        functools.partial(finish_kernel, mine),
        out_shape=jax.ShapeDtypeStruct((SLAB, HALF), BF16),
        in_specs=[SMEM] + [VMEM] * 8,
        out_specs=VMEM,
        compiler_params=pltpu.CompilerParams(vmem_limit_bytes=32 * 2**20),
        cost_estimate=pl.CostEstimate(
            flops=4 * SLAB * HDIM * HDIM, bytes_accessed=2 * 2**20, transcendentals=0
        ),
    )(*args)


def after(value, *others):
    return lax.optimization_barrier((value, others))[0]


def pace_kernel(piece, out):
    pass


def pace(piece):
    return pl.pallas_call(
        pace_kernel,
        out_shape=jax.ShapeDtypeStruct(piece.shape, piece.dtype),
        in_specs=[ANY],
        out_specs=ANY,
        input_output_aliases={0: 0},
        compiler_params=pltpu.CompilerParams(vmem_limit_bytes=2**20),
        cost_estimate=pl.CostEstimate(flops=2500000000, bytes_accessed=0, transcendentals=0),
    )(piece)


def gather(tokens, weights, core):
    even = jnp.concatenate([tokens[:, :ROWS], tokens[:, 2 * ROWS : 3 * ROWS]], axis=1)
    odd = jnp.concatenate([tokens[:, ROWS : 2 * ROWS], tokens[:, 3 * ROWS :]], axis=1)
    own = jnp.where(core == 0, even, odd)
    theirs = lax.ppermute(jnp.where(core == 0, odd, even), "seq", SWAP)
    ring = ring_pairs()

    def pass_on(piece):
        return lax.ppermute(piece, ("seq", "head"), ring)

    first, second = [own], [theirs]
    for k in range(1, Z):
        for stream in (first, second):
            piece = stream[-1]
            stream.append(pace(pass_on(piece)))
    streams = list(weights)
    got = [None, None]
    blocks = []
    for step in range(4):
        if step:
            if (0, 0, 0, 0)[step]:
                got = after(got, first[(0, 0, 0, 0)[step]])
            streams = [jnp.concatenate(pair, axis=0) for pair in zip(streams, got)]
        got = [lax.ppermute(streams[j], "seq", cube_pairs(j, step)) for j in range(2)]
    for j in range(2):
        blocks += [streams[j], got[j]]
    pieces = zip(first, second)
    return [p for pair in pieces for p in pair], blocks


def local(tokens, w_query, w_key, w_value, gain):
    seq = lax.axis_index("seq")
    core = seq % C
    x = (seq // C) % X
    info = jnp.concatenate(
        [
            core[None].astype(jnp.int32),
            jnp.asarray(place_table())[seq * Z + lax.axis_index("head")],
        ]
    )
    halves = [
        jnp.concatenate([w[:, j * HALF : (j + 1) * HALF] for w in (w_key, w_value, w_query)], axis=1)
        for j in range(2)
    ]
    pieces, blocks = gather(tokens, halves, core)

    (kv_theirs,) = product(info, pieces, blocks, ((False, 0, 2 * HALF),))
    kv_got = lax.ppermute(kv_theirs, "seq", SWAP)
    (kv_mine,) = product(info, pieces, blocks, ((True, 0, 2 * HALF),))
    key, value, within, total = pair_states(kv_mine, kv_got)

    row = total.astype(F32)
    before = jnp.zeros_like(row)
    for k in range(1, X):
        got = lax.ppermute(total, "seq", spin_x(k)).astype(F32)
        row = row + got
        before = before + jnp.where(x >= k, got, 0.0)
    row = row.astype(BF16)
    rows = [lax.ppermute(row, "seq", shift_y(k)) for k in range(1, Y)]

    q_theirs, q_mine = product(
        after(info, total), pieces, blocks, ((False, 2 * HALF, 3 * HALF), (True, 2 * HALF, 3 * HALF))
    )
    q_got = lax.ppermute(q_theirs, "seq", SWAP)
    query, inside = local_part(q_mine, q_got, key, value)

    gain_here = lax.dynamic_slice(gain, (core * HALF,), (HALF,)).reshape(1, HALF)
    last = (info, query, inside, within, before, *rows, gain_here)
    out_got = lax.ppermute(finish(False, *last), "seq", SWAP)
    out_mine = finish(True, *last)
    return jnp.concatenate(
        [jnp.where(core == 0, out_mine, out_got), jnp.where(core == 0, out_got, out_mine)], axis=1
    )


def solution(mesh):
    in_specs = (P("seq", "head"), P("seq", "head"), P("seq", "head"), P("seq", "head"), P("head"))
    out_specs = P("seq", "head")
    return jax.shard_map(local, mesh=mesh, in_specs=in_specs, out_specs=out_specs, check_vma=False)
```

```python
import functools

import jax
import jax.numpy as jnp
import numpy as np
from jax import lax
from jax.experimental import pallas as pl
from jax.experimental.pallas import tpu as pltpu
from jax.sharding import PartitionSpec as P

HDIM = 128
SPAN = 256
Y, X, C, Z = 4, 4, 2, 8
ROWS = 192
PIECE = 2 * ROWS
SLAB = 512
CHIP = C * SLAB
HALF = 256
BLOCKS = 4
F32, BF16 = jnp.float32, jnp.bfloat16
DIMS = (
    lambda y, x: (y, x ^ 1),
    lambda y, x: (y ^ 1, x),
    lambda y, x: (y, x ^ 3),
    lambda y, x: (y ^ 3, x),
)
ANY = pl.BlockSpec(memory_space=pl.ANY)
VMEM = pl.BlockSpec(memory_space=pltpu.VMEM)
SMEM = pl.BlockSpec(memory_space=pltpu.SMEM)


def seq_of(y, x, c):
    return (y * X + x) * C + c


def chips():
    return [(y, x) for y in range(Y) for x in range(X)]


def dim_of(stream, core, step):
    return (2 * stream + core + step) % 4


def cube_pairs(stream, step):
    return [
        (seq_of(y, x, c), seq_of(*DIMS[dim_of(stream, c, step)](y, x), c))
        for y, x in chips()
        for c in range(C)
    ]


def ring_pairs():
    return [
        (s * Z + z, s * Z + (z + (1 if s % C == 0 else -1)) % Z)
        for s in range(Y * X * C)
        for z in range(Z)
    ]


SWAP = [(s, s ^ 1) for s in range(Y * X * C)]


def spin_x(k):
    return [(seq_of(y, x, c), seq_of(y, (x + k) % X, c)) for y, x in chips() for c in range(C)]


def shift_y(k):
    return [
        (seq_of(y, x, c), seq_of(y + k, x, c)) for y, x in chips() for c in range(C) if y + k < Y
    ]


def place_table():
    table = np.zeros((Y * X * C, Z, 2 + 4 * Z), np.int32)
    for y, x in chips():
        for c in range(C):
            for z in range(Z):
                places = []
                for stream in range(2):
                    for k in range(Z):
                        for e in range(2):
                            source = 2 * ((z - k if c == 0 else z + k) % Z) + e
                            dx, dy = (source % X) ^ x, (source // X) ^ y
                            bits = (
                                (dx & 1) ^ (dx >> 1),
                                (dy & 1) ^ (dy >> 1),
                                dx >> 1,
                                dy >> 1,
                            )
                            places.append(
                                sum(bits[dim_of(stream, c, step)] << step for step in range(4))
                            )
                table[seq_of(y, x, c), z] = [c, x] + places
    return table.reshape(Y * X * C * Z, 2 + 4 * Z)


def silu(u):
    return u / (1.0 + jnp.exp(-u))


def product_kernel(parts, info, *refs):
    tokens, refs = refs[: 2 * Z], refs[2 * Z :]
    weights, refs = refs[: 2 * BLOCKS], refs[2 * BLOCKS :]
    outs, (piled,) = refs[: len(parts)], refs[len(parts) :]
    core = info[0]
    deep = 2 * PIECE
    for part, (mine, low, high) in enumerate(parts):
        half = core if mine else 1 - core

        @pl.loop(0, 2 * Z)
        def _(at):
            place = info[2 + half * 2 * Z + at]
            source = pl.ds(pl.multiple_of((place % 4) * ROWS, ROWS), ROWS)
            target = pl.ds(pl.multiple_of(at * ROWS, ROWS), ROWS)
            choice = half * BLOCKS + place // 4
            for b in range(2 * BLOCKS):

                @pl.when(choice == b)
                def _():
                    piled[target, 0 : high - low] = weights[b][source, low:high]

        for slab in range(2):
            first = pl.multiple_of(SLAB * (core if slab == 0 else 1 - core), SLAB)
            for n in range(0, high - low, 256):
                total = None
                for k in range(0, Z, 2):
                    piece = jnp.concatenate(
                        [tokens[2 * k + slab][...], tokens[2 * k + 2 + slab][...]], axis=1
                    )
                    some = jnp.dot(
                        piece,
                        piled[k * PIECE : k * PIECE + deep, n : n + 256],
                        preferred_element_type=F32,
                    )
                    total = some if total is None else total + some
                outs[part][pl.ds(first, SLAB), n : n + 256] = total.astype(outs[part].dtype)


def product(info, tokens, weights, parts):
    wide = max(high - low for _, low, high in parts)
    flops = sum(2 * CHIP * Z * PIECE * (high - low) for _, low, high in parts)
    return pl.pallas_call(
        functools.partial(product_kernel, parts),
        out_shape=[
            jax.ShapeDtypeStruct((CHIP, high - low), F32 if mine else BF16)
            for mine, low, high in parts
        ],
        in_specs=[SMEM] + [VMEM] * (2 * Z + 2 * BLOCKS),
        out_specs=[VMEM] * len(parts),
        scratch_shapes=[pltpu.VMEM((Z * PIECE, wide), BF16)],
        compiler_params=pltpu.CompilerParams(vmem_limit_bytes=20 * 2**20),
        cost_estimate=pl.CostEstimate(
            flops=flops, bytes_accessed=16 * 2**20, transcendentals=0
        ),
    )(info, *tokens, *weights)


def pairs_kernel(mine, other, key, value, within, total):
    for h in range(2):
        running = jnp.zeros((HDIM, HDIM), F32)
        for b in range(CHIP // SPAN):
            rows = slice(b * SPAN, (b + 1) * SPAN)
            got = []
            for at, out in ((0, key), (HALF, value)):
                cols = slice(at + h * HDIM, at + (h + 1) * HDIM)
                u = mine[rows, cols] + other[rows, cols].astype(F32)
                got.append(silu(u).astype(BF16))
                out[rows, h * HDIM : (h + 1) * HDIM] = got[-1]
            within[b, h] = running
            running = running + lax.dot_general(
                *got, (((0,), (0,)), ((), ())), preferred_element_type=F32
            )
        total[h] = running.astype(BF16)


def pair_states(mine, other):
    return pl.pallas_call(
        pairs_kernel,
        out_shape=[
            jax.ShapeDtypeStruct((CHIP, HALF), BF16),
            jax.ShapeDtypeStruct((CHIP, HALF), BF16),
            jax.ShapeDtypeStruct((CHIP // SPAN, 2, HDIM, HDIM), F32),
            jax.ShapeDtypeStruct((2, HDIM, HDIM), BF16),
        ],
        in_specs=[VMEM] * 2,
        out_specs=[VMEM] * 4,
        compiler_params=pltpu.CompilerParams(vmem_limit_bytes=12 * 2**20),
        cost_estimate=pl.CostEstimate(
            flops=2 * CHIP * 2 * HDIM * HDIM, bytes_accessed=5 * 2**20, transcendentals=CHIP * 512
        ),
    )(mine, other)


def row_kernel(info, total, left_1, left_2, left_3, row, before):
    x = info[1]
    whole = total[...].astype(F32)
    earlier = jnp.zeros_like(whole)
    for k, left in enumerate((left_1, left_2, left_3), 1):
        got = left[...].astype(F32)
        whole = whole + got
        earlier = earlier + jnp.where(x >= k, got, 0.0)
    row[...] = whole.astype(BF16)
    before[...] = earlier


def row_sums(info, total, *from_left):
    return pl.pallas_call(
        row_kernel,
        out_shape=[
            jax.ShapeDtypeStruct(total.shape, BF16),
            jax.ShapeDtypeStruct(total.shape, F32),
        ],
        in_specs=[SMEM] + [VMEM] * 4,
        out_specs=[VMEM] * 2,
        compiler_params=pltpu.CompilerParams(vmem_limit_bytes=4 * 2**20),
        cost_estimate=pl.CostEstimate(flops=2**18, bytes_accessed=2**19, transcendentals=0),
    )(info, total, *from_left)


def local_kernel(mine, other, key, value, query, inside):
    causal = lax.broadcasted_iota(jnp.int32, (SPAN, SPAN), 0) >= lax.broadcasted_iota(
        jnp.int32, (SPAN, SPAN), 1
    )
    for b in range(CHIP // SPAN):
        for h in range(2):
            at = (slice(b * SPAN, (b + 1) * SPAN), slice(h * HDIM, (h + 1) * HDIM))
            q = silu(mine[at] + other[at].astype(F32)).astype(BF16)
            query[at] = q
            scores = lax.dot_general(
                q, key[at], (((1,), (1,)), ((), ())), preferred_element_type=F32
            )
            scores = jnp.where(causal, scores, 0.0).astype(BF16)
            inside[at] = jnp.dot(scores, value[at], preferred_element_type=F32)


def local_part(mine, other, key, value):
    return pl.pallas_call(
        local_kernel,
        out_shape=[
            jax.ShapeDtypeStruct((CHIP, HALF), BF16),
            jax.ShapeDtypeStruct((CHIP, HALF), F32),
        ],
        in_specs=[VMEM] * 4,
        out_specs=[VMEM] * 2,
        compiler_params=pltpu.CompilerParams(vmem_limit_bytes=12 * 2**20),
        cost_estimate=pl.CostEstimate(
            flops=8 * CHIP * SPAN * HDIM, bytes_accessed=5 * 2**20, transcendentals=CHIP * HALF
        ),
    )(mine, other, key, value)


def finish_kernel(mine, info, query, inside, within, before, rows_0, rows_1, rows_2, gain, out):
    core = info[0]
    first = core if mine else 1 - core
    for h in range(2):
        cols = slice(h * HDIM, (h + 1) * HDIM)
        earlier = before[h]
        for rows in (rows_0, rows_1, rows_2):
            earlier = earlier + rows[h].astype(F32)
        for b in range(SLAB // SPAN):
            at = pl.ds(pl.multiple_of(first * SLAB + b * SPAN, SPAN), SPAN)
            state = (earlier + within[first * (SLAB // SPAN) + b, h]).astype(BF16)
            attended = inside[at, cols] + jnp.dot(
                query[at, cols], state, preferred_element_type=F32
            )
            scale = lax.rsqrt(jnp.mean(attended * attended, axis=-1, keepdims=True) + 1e-06)
            out[b * SPAN : (b + 1) * SPAN, cols] = (attended * scale * gain[:, cols]).astype(BF16)


def finish(mine, *args):
    return pl.pallas_call(
        functools.partial(finish_kernel, mine),
        out_shape=jax.ShapeDtypeStruct((SLAB, HALF), BF16),
        in_specs=[SMEM] + [VMEM] * 8,
        out_specs=VMEM,
        compiler_params=pltpu.CompilerParams(vmem_limit_bytes=12 * 2**20),
        cost_estimate=pl.CostEstimate(
            flops=4 * SLAB * HDIM * HDIM, bytes_accessed=2 * 2**20, transcendentals=0
        ),
    )(*args)


def after(value, *others):
    return lax.optimization_barrier((value, others))[0]


def pace_kernel(piece, out):
    pass


def pace(piece):
    return pl.pallas_call(
        pace_kernel,
        out_shape=jax.ShapeDtypeStruct(piece.shape, piece.dtype),
        in_specs=[ANY],
        out_specs=ANY,
        input_output_aliases={0: 0},
        compiler_params=pltpu.CompilerParams(vmem_limit_bytes=2**20),
        cost_estimate=pl.CostEstimate(flops=2750000000, bytes_accessed=0, transcendentals=0),
    )(piece)


def gather(tokens, weights, core):
    even = jnp.concatenate([tokens[:, :ROWS], tokens[:, 2 * ROWS : 3 * ROWS]], axis=1)
    odd = jnp.concatenate([tokens[:, ROWS : 2 * ROWS], tokens[:, 3 * ROWS :]], axis=1)
    own = jnp.where(core == 0, even, odd)
    theirs = lax.ppermute(jnp.where(core == 0, odd, even), "seq", SWAP)
    ring = ring_pairs()

    def pass_on(piece):
        return lax.ppermute(piece, ("seq", "head"), ring)

    first, second = [own], [theirs]
    for k in range(1, Z):
        for stream in (first, second):
            piece = stream[-1]
            stream.append(pace(pass_on(piece)))
    streams = list(weights)
    got = [None, None]
    for step in range(3):
        if step:
            streams = [jnp.concatenate(pair, axis=0) for pair in zip(streams, got)]
        got = [lax.ppermute(streams[j], "seq", cube_pairs(j, step)) for j in range(2)]
    blocks = []
    for j in range(2):
        blocks += [streams[j], got[j]]
        blocks += [lax.ppermute(part, "seq", cube_pairs(j, 3)) for part in (streams[j], got[j])]
    pieces = zip(first, second)
    return [p for pair in pieces for p in pair], blocks


def local(tokens, w_query, w_key, w_value, gain):
    seq = lax.axis_index("seq")
    core = seq % C
    table = jnp.asarray(place_table())
    info = lax.dynamic_slice(table, (seq * Z + lax.axis_index("head"), 0), (1, table.shape[1]))[0]
    gain_here = lax.dynamic_slice(gain, (core * HALF,), (HALF,)).reshape(1, HALF)
    tokens, info, gain_here = lax.optimization_barrier((tokens, info, gain_here))
    halves = [
        jnp.concatenate([w[:, j * HALF : (j + 1) * HALF] for w in (w_key, w_value, w_query)], axis=1)
        for j in range(2)
    ]
    pieces, blocks = gather(tokens, halves, core)

    (kv_theirs,) = product(info, pieces, blocks, ((False, 0, 2 * HALF),))
    kv_got = lax.ppermute(kv_theirs, "seq", SWAP)
    (kv_mine,) = product(info, pieces, blocks, ((True, 0, 2 * HALF),))
    key, value, within, total = pair_states(kv_mine, kv_got)

    from_left = [lax.ppermute(total, "seq", spin_x(k)) for k in range(1, X)]
    (q_theirs,) = product(
        after(info, total), pieces, blocks, ((False, 2 * HALF, 3 * HALF),)
    )
    q_got = lax.ppermute(q_theirs, "seq", SWAP)
    row, before = row_sums(info, after(total, q_theirs), *from_left)
    rows = [lax.ppermute(row, "seq", shift_y(k)) for k in range(1, Y)]
    (q_mine,) = product(after(info, row), pieces, blocks, ((True, 2 * HALF, 3 * HALF),))
    query, inside = local_part(q_mine, q_got, key, value)

    last = (info, query, inside, within, before, *rows, gain_here)
    out_got = lax.ppermute(finish(False, *last), "seq", SWAP)
    out_mine = finish(True, *last)
    return jnp.concatenate(
        [jnp.where(core == 0, out_mine, out_got), jnp.where(core == 0, out_got, out_mine)], axis=1
    )


def solution(mesh):
    in_specs = (P("seq", "head"), P("seq", "head"), P("seq", "head"), P("seq", "head"), P("head"))
    out_specs = P("seq", "head")
    return jax.shard_map(local, mesh=mesh, in_specs=in_specs, out_specs=out_specs, check_vma=False)
```

```python
import functools

import jax
import jax.numpy as jnp
import numpy as np
from jax import lax
from jax.experimental import pallas as pl
from jax.experimental.pallas import tpu as pltpu
from jax.sharding import PartitionSpec as P

HDIM = 128
SPAN = 256
Y, X, C, Z = 4, 4, 2, 8
ROWS = 192
PIECE = 2 * ROWS
SLAB = 512
CHIP = C * SLAB
HALF = 256
BLOCKS = 2
F32, BF16 = jnp.float32, jnp.bfloat16
DIMS = (
    lambda y, x: (y, x ^ 1),
    lambda y, x: (y ^ 1, x),
    lambda y, x: (y, x ^ 3),
    lambda y, x: (y ^ 3, x),
)
ANY = pl.BlockSpec(memory_space=pl.ANY)
VMEM = pl.BlockSpec(memory_space=pltpu.VMEM)
SMEM = pl.BlockSpec(memory_space=pltpu.SMEM)


def seq_of(y, x, c):
    return (y * X + x) * C + c


def chips():
    return [(y, x) for y in range(Y) for x in range(X)]


def dim_of(stream, core, step):
    return (2 * stream + core + step) % 4


def cube_pairs(stream, step):
    return [
        (seq_of(y, x, c), seq_of(*DIMS[dim_of(stream, c, step)](y, x), c))
        for y, x in chips()
        for c in range(C)
    ]


def ring_pairs():
    return [
        (s * Z + z, s * Z + (z + (1 if s % C == 0 else -1)) % Z)
        for s in range(Y * X * C)
        for z in range(Z)
    ]


SWAP = [(s, s ^ 1) for s in range(Y * X * C)]


def spin_x(k):
    return [(seq_of(y, x, c), seq_of(y, (x + k) % X, c)) for y, x in chips() for c in range(C)]


def shift_y(k):
    return [
        (seq_of(y, x, c), seq_of(y + k, x, c)) for y, x in chips() for c in range(C) if y + k < Y
    ]


def place_table():
    table = np.zeros((Y * X * C, Z, 2 + 4 * Z), np.int32)
    for y, x in chips():
        for c in range(C):
            for z in range(Z):
                places = []
                for stream in range(2):
                    for k in range(Z):
                        for e in range(2):
                            source = 2 * ((z - k if c == 0 else z + k) % Z) + e
                            dx, dy = (source % X) ^ x, (source // X) ^ y
                            bits = (
                                (dx & 1) ^ (dx >> 1),
                                (dy & 1) ^ (dy >> 1),
                                dx >> 1,
                                dy >> 1,
                            )
                            places.append(
                                sum(bits[dim_of(stream, c, step)] << step for step in range(4))
                            )
                table[seq_of(y, x, c), z] = [c, x] + places
    return table.reshape(Y * X * C * Z, 2 + 4 * Z)


def silu(u):
    return u / (1.0 + jnp.exp(-u))


def product_kernel(mine, low, high, info, *refs):
    tokens, weights, (out, piled) = refs[: 2 * Z], refs[2 * Z : 2 * Z + BLOCKS], refs[-2:]
    core = info[0]
    for slab in range(2):
        first = pl.multiple_of(SLAB * (core if slab == 0 else 1 - core), SLAB)
        total = None
        for k in range(0, Z, 2):
            deep = slice(k * PIECE, (k + 2) * PIECE)
            if slab == 0:
                for at in range(2 * k, 2 * k + 4):
                    place = info[2 + mine * 2 * Z + at]
                    row = pl.ds(pl.multiple_of((place % 8) * ROWS, ROWS), ROWS)
                    one, two = (w[row, low:high] for w in weights)
                    piled[at * ROWS : (at + 1) * ROWS] = jnp.where(place < 8, one, two)
            piece = jnp.concatenate(
                [tokens[2 * k + slab][...], tokens[2 * k + 2 + slab][...]], axis=1
            )
            some = jnp.dot(piece, piled[deep], preferred_element_type=F32)
            total = some if total is None else total + some
        out[pl.ds(first, SLAB), :] = total.astype(out.dtype)


def product(info, tokens, blocks, mine, low, high):
    return pl.pallas_call(
        functools.partial(product_kernel, mine, low, high),
        out_shape=jax.ShapeDtypeStruct((CHIP, high - low), F32 if mine else BF16),
        in_specs=[SMEM] + [VMEM] * (2 * Z + BLOCKS),
        out_specs=VMEM,
        scratch_shapes=[pltpu.VMEM((Z * PIECE, high - low), BF16)],
        compiler_params=pltpu.CompilerParams(vmem_limit_bytes=20 * 2**20),
        cost_estimate=pl.CostEstimate(
            flops=2 * CHIP * Z * PIECE * (high - low), bytes_accessed=2**20, transcendentals=0
        ),
    )(info, *tokens, *blocks[mine])


def pairs_kernel(mine, other, key, value, within, total):
    for h in range(2):
        running = jnp.zeros((HDIM, HDIM), F32)
        for b in range(CHIP // SPAN):
            rows = slice(b * SPAN, (b + 1) * SPAN)
            got = []
            for at, out in ((0, key), (HALF, value)):
                cols = slice(at + h * HDIM, at + (h + 1) * HDIM)
                u = mine[rows, cols] + other[rows, cols].astype(F32)
                got.append(silu(u).astype(BF16))
                out[rows, h * HDIM : (h + 1) * HDIM] = got[-1]
            within[b, h] = running
            running = running + lax.dot_general(
                *got, (((0,), (0,)), ((), ())), preferred_element_type=F32
            )
        total[h] = running.astype(BF16)


def pair_states(mine, other):
    return pl.pallas_call(
        pairs_kernel,
        out_shape=[
            jax.ShapeDtypeStruct((CHIP, HALF), BF16),
            jax.ShapeDtypeStruct((CHIP, HALF), BF16),
            jax.ShapeDtypeStruct((CHIP // SPAN, 2, HDIM, HDIM), F32),
            jax.ShapeDtypeStruct((2, HDIM, HDIM), BF16),
        ],
        in_specs=[VMEM] * 2,
        out_specs=[VMEM] * 4,
        compiler_params=pltpu.CompilerParams(vmem_limit_bytes=12 * 2**20),
        cost_estimate=pl.CostEstimate(
            flops=2 * CHIP * 2 * HDIM * HDIM, bytes_accessed=5 * 2**20, transcendentals=CHIP * 512
        ),
    )(mine, other)


def row_kernel(info, total, left_1, left_2, left_3, row, before):
    x = info[1]
    whole = total[...].astype(F32)
    earlier = jnp.zeros_like(whole)
    for k, left in enumerate((left_1, left_2, left_3), 1):
        got = left[...].astype(F32)
        whole = whole + got
        earlier = earlier + jnp.where(x >= k, got, 0.0)
    row[...] = whole.astype(BF16)
    before[...] = earlier


def row_sums(info, total, *from_left):
    return pl.pallas_call(
        row_kernel,
        out_shape=[
            jax.ShapeDtypeStruct(total.shape, BF16),
            jax.ShapeDtypeStruct(total.shape, F32),
        ],
        in_specs=[SMEM] + [VMEM] * 4,
        out_specs=[VMEM] * 2,
        compiler_params=pltpu.CompilerParams(vmem_limit_bytes=4 * 2**20),
        cost_estimate=pl.CostEstimate(flops=2**18, bytes_accessed=2**19, transcendentals=0),
    )(info, total, *from_left)


def local_kernel(mine, other, key, value, query, inside):
    causal = lax.broadcasted_iota(jnp.int32, (SPAN, SPAN), 0) >= lax.broadcasted_iota(
        jnp.int32, (SPAN, SPAN), 1
    )
    for b in range(CHIP // SPAN):
        for h in range(2):
            at = (slice(b * SPAN, (b + 1) * SPAN), slice(h * HDIM, (h + 1) * HDIM))
            q = silu(mine[at] + other[at].astype(F32)).astype(BF16)
            query[at] = q
            scores = lax.dot_general(
                q, key[at], (((1,), (1,)), ((), ())), preferred_element_type=F32
            )
            scores = jnp.where(causal, scores, 0.0).astype(BF16)
            inside[at] = jnp.dot(scores, value[at], preferred_element_type=F32)


def local_part(mine, other, key, value):
    return pl.pallas_call(
        local_kernel,
        out_shape=[
            jax.ShapeDtypeStruct((CHIP, HALF), BF16),
            jax.ShapeDtypeStruct((CHIP, HALF), F32),
        ],
        in_specs=[VMEM] * 4,
        out_specs=[VMEM] * 2,
        compiler_params=pltpu.CompilerParams(vmem_limit_bytes=12 * 2**20),
        cost_estimate=pl.CostEstimate(
            flops=8 * CHIP * SPAN * HDIM, bytes_accessed=5 * 2**20, transcendentals=CHIP * HALF
        ),
    )(mine, other, key, value)


def finish_kernel(mine, info, query, inside, within, before, rows_0, rows_1, rows_2, gain, out):
    core = info[0]
    first = core if mine else 1 - core
    for h in range(2):
        cols = slice(h * HDIM, (h + 1) * HDIM)
        gain_here = gain[:, pl.ds(pl.multiple_of(core * HALF + h * HDIM, HDIM), HDIM)]
        earlier = before[h]
        for rows in (rows_0, rows_1, rows_2):
            earlier = earlier + rows[h].astype(F32)
        for b in range(SLAB // SPAN):
            at = pl.ds(pl.multiple_of(first * SLAB + b * SPAN, SPAN), SPAN)
            state = (earlier + within[first * (SLAB // SPAN) + b, h]).astype(BF16)
            attended = inside[at, cols] + jnp.dot(
                query[at, cols], state, preferred_element_type=F32
            )
            scale = lax.rsqrt(jnp.mean(attended * attended, axis=-1, keepdims=True) + 1e-06)
            out[b * SPAN : (b + 1) * SPAN, cols] = (attended * scale * gain_here).astype(BF16)


def finish(mine, *args):
    return pl.pallas_call(
        functools.partial(finish_kernel, mine),
        out_shape=jax.ShapeDtypeStruct((SLAB, HALF), BF16),
        in_specs=[SMEM] + [VMEM] * 8,
        out_specs=VMEM,
        compiler_params=pltpu.CompilerParams(vmem_limit_bytes=12 * 2**20),
        cost_estimate=pl.CostEstimate(
            flops=4 * SLAB * HDIM * HDIM, bytes_accessed=2 * 2**20, transcendentals=0
        ),
    )(*args)


def after(value, *others):
    return lax.optimization_barrier((value, others))[0]


def pace_kernel(piece, out):
    pass


def pace(piece):
    return pl.pallas_call(
        pace_kernel,
        out_shape=jax.ShapeDtypeStruct(piece.shape, piece.dtype),
        in_specs=[ANY],
        out_specs=ANY,
        input_output_aliases={0: 0},
        compiler_params=pltpu.CompilerParams(vmem_limit_bytes=2**20),
        cost_estimate=pl.CostEstimate(flops=2500000000, bytes_accessed=0, transcendentals=0),
    )(piece)


def gather(tokens, weights, core):
    even = jnp.concatenate([tokens[:, :ROWS], tokens[:, 2 * ROWS : 3 * ROWS]], axis=1)
    odd = jnp.concatenate([tokens[:, ROWS : 2 * ROWS], tokens[:, 3 * ROWS :]], axis=1)
    own = jnp.where(core == 0, even, odd)
    theirs = lax.ppermute(jnp.where(core == 0, odd, even), "seq", SWAP)
    ring = ring_pairs()

    def pass_on(piece):
        return lax.ppermute(piece, ("seq", "head"), ring)

    first, second = [own], [theirs]
    for k in range(1, Z):
        for stream in (first, second):
            piece = stream[-1]
            stream.append(pace(pass_on(piece)))
    streams = list(weights)
    got = [None, None]
    for step in range(4):
        if step:
            streams = [jnp.concatenate(pair, axis=0) for pair in zip(streams, got)]
        got = [lax.ppermute(streams[j], "seq", cube_pairs(j, step)) for j in range(2)]
    blocks = [[streams[j], got[j]] for j in range(2)]
    pieces = zip(first, second)
    return [p for pair in pieces for p in pair], blocks


def local(tokens, w_query, w_key, w_value, gain):
    index = (lax.axis_index("seq") * Z + lax.axis_index("head")).astype(jnp.uint32)
    core = (lax.axis_index("seq").astype(jnp.uint32)) % C
    tokens, index, core = lax.optimization_barrier((tokens, index, core))
    table = jnp.asarray(place_table())
    info = lax.dynamic_slice(table, (index, jnp.uint32(0)), (1, table.shape[1]))[0]
    low, high = (
        jnp.concatenate([w[:, j * HALF : (j + 1) * HALF] for w in (w_key, w_value, w_query)], axis=1)
        for j in range(2)
    )
    halves = [jnp.where(core == 0, high, low), jnp.where(core == 0, low, high)]
    pieces, blocks = gather(tokens, halves, core)

    kv_theirs = product(info, pieces, blocks, 0, 0, 2 * HALF)
    kv_got = lax.ppermute(kv_theirs, "seq", SWAP)
    kv_mine = product(info, pieces, blocks, 1, 0, 2 * HALF)
    key, value, within, total = pair_states(kv_mine, kv_got)

    from_left = [lax.ppermute(total, "seq", spin_x(k)) for k in range(1, X)]
    q_theirs = product(after(info, total), pieces, blocks, 0, 2 * HALF, 3 * HALF)
    q_got = lax.ppermute(q_theirs, "seq", SWAP)
    row, before = row_sums(info, after(total, q_theirs), *from_left)
    rows = [lax.ppermute(row, "seq", shift_y(k)) for k in range(1, Y)]
    q_mine = product(after(info, row), pieces, blocks, 1, 2 * HALF, 3 * HALF)
    query, inside = local_part(q_mine, q_got, key, value)

    last = (info, query, inside, within, before, *rows, gain.reshape(1, 2 * HALF))
    out_got = lax.ppermute(finish(False, *last), "seq", SWAP)
    out_mine = finish(True, *last)
    return jnp.concatenate(
        [jnp.where(core == 0, out_mine, out_got), jnp.where(core == 0, out_got, out_mine)], axis=1
    )


def solution(mesh):
    in_specs = (P("seq", "head"), P("seq", "head"), P("seq", "head"), P("seq", "head"), P("head"))
    out_specs = P("seq", "head")
    return jax.shard_map(local, mesh=mesh, in_specs=in_specs, out_specs=out_specs, check_vma=False)
```

```python
import functools

import jax
import jax.numpy as jnp
import numpy as np
from jax import lax
from jax.experimental import pallas as pl
from jax.experimental.pallas import tpu as pltpu
from jax.sharding import PartitionSpec as P

HDIM = 128
SPAN = 256
Y, X, C, Z = 4, 4, 2, 8
ROWS = 192
PIECE = 2 * ROWS
SLAB = 512
CHIP = C * SLAB
HALF = 256
PLACES = 5
BLOCKS = 2
F32, BF16 = jnp.float32, jnp.bfloat16
DIMS = (
    lambda y, x: (y, x ^ 1),
    lambda y, x: (y ^ 1, x),
    lambda y, x: (y, x ^ 3),
    lambda y, x: (y ^ 3, x),
)
ANY = pl.BlockSpec(memory_space=pl.ANY)
VMEM = pl.BlockSpec(memory_space=pltpu.VMEM)
SMEM = pl.BlockSpec(memory_space=pltpu.SMEM)


def seq_of(y, x, c):
    return (y * X + x) * C + c


def chips():
    return [(y, x) for y in range(Y) for x in range(X)]


def dim_of(stream, core, step):
    return (2 * stream + core + step) % 4


def cube_pairs(stream, step):
    return [
        (seq_of(y, x, c), seq_of(*DIMS[dim_of(stream, c, step)](y, x), c))
        for y, x in chips()
        for c in range(C)
    ]


def ring_pairs():
    return [
        (s * Z + z, s * Z + (z + (1 if s % C == 0 else -1)) % Z)
        for s in range(Y * X * C)
        for z in range(Z)
    ]


SWAP = [(s, s ^ 1) for s in range(Y * X * C)]


def exchange_pairs(dim):
    return [(seq_of(y, x, c), seq_of(*DIMS[dim](y, x), c)) for y, x in chips() for c in range(C)]


def place_table():
    table = np.zeros((Y * X * C, Z, PLACES + 4 * Z), np.int32)
    for y, x in chips():
        for c in range(C):
            for z in range(Z):
                places = []
                for stream in range(2):
                    for k in range(Z):
                        for e in range(2):
                            source = 2 * ((z - k if c == 0 else z + k) % Z) + e
                            dx, dy = (source % X) ^ x, (source // X) ^ y
                            bits = (
                                (dx & 1) ^ (dx >> 1),
                                (dy & 1) ^ (dy >> 1),
                                dx >> 1,
                                dy >> 1,
                            )
                            places.append(
                                sum(bits[dim_of(stream, c, step)] << step for step in range(4))
                            )
                after_partner = [x & 1, x >> 1, y & 1, y >> 1]
                table[seq_of(y, x, c), z] = [c] + after_partner + places
    return table.reshape(Y * X * C * Z, PLACES + 4 * Z)


def silu(u):
    return u / (1.0 + jnp.exp(-u))


def product_kernel(mine, low, high, info, *refs):
    tokens, weights, (out, piled) = refs[: 2 * Z], refs[2 * Z : 2 * Z + BLOCKS], refs[-2:]
    core = info[0]
    for slab in range(2):
        first = pl.multiple_of(SLAB * (core if slab == 0 else 1 - core), SLAB)
        total = None
        for k in range(0, Z, 2):
            deep = slice(k * PIECE, (k + 2) * PIECE)
            if slab == 0:
                for at in range(2 * k, 2 * k + 4):
                    place = info[PLACES + mine * 2 * Z + at]
                    row = pl.ds(pl.multiple_of((place % 8) * ROWS, ROWS), ROWS)
                    one, two = (w[row, low:high] for w in weights)
                    piled[at * ROWS : (at + 1) * ROWS] = jnp.where(place < 8, one, two)
            piece = jnp.concatenate(
                [tokens[2 * k + slab][...], tokens[2 * k + 2 + slab][...]], axis=1
            )
            some = jnp.dot(piece, piled[deep], preferred_element_type=F32)
            total = some if total is None else total + some
        out[pl.ds(first, SLAB), :] = total.astype(out.dtype)


def product(info, tokens, blocks, mine, low, high):
    return pl.pallas_call(
        functools.partial(product_kernel, mine, low, high),
        out_shape=jax.ShapeDtypeStruct((CHIP, high - low), F32 if mine else BF16),
        in_specs=[SMEM] + [VMEM] * (2 * Z + BLOCKS),
        out_specs=VMEM,
        scratch_shapes=[pltpu.VMEM((Z * PIECE, high - low), BF16)],
        compiler_params=pltpu.CompilerParams(vmem_limit_bytes=20 * 2**20),
        cost_estimate=pl.CostEstimate(
            flops=2 * CHIP * Z * PIECE * (high - low), bytes_accessed=2**20, transcendentals=0
        ),
    )(info, *tokens, *blocks[mine])


def pairs_kernel(mine, other, key, value, within, total):
    for h in range(2):
        running = jnp.zeros((HDIM, HDIM), F32)
        for b in range(CHIP // SPAN):
            rows = slice(b * SPAN, (b + 1) * SPAN)
            got = []
            for at, out in ((0, key), (HALF, value)):
                cols = slice(at + h * HDIM, at + (h + 1) * HDIM)
                u = mine[rows, cols] + other[rows, cols].astype(F32)
                got.append(silu(u).astype(BF16))
                out[rows, h * HDIM : (h + 1) * HDIM] = got[-1]
            within[b, h] = running
            running = running + lax.dot_general(
                *got, (((0,), (0,)), ((), ())), preferred_element_type=F32
            )
        total[h] = running.astype(BF16)


def pair_states(mine, other):
    return pl.pallas_call(
        pairs_kernel,
        out_shape=[
            jax.ShapeDtypeStruct((CHIP, HALF), BF16),
            jax.ShapeDtypeStruct((CHIP, HALF), BF16),
            jax.ShapeDtypeStruct((CHIP // SPAN, 2, HDIM, HDIM), F32),
            jax.ShapeDtypeStruct((2, HDIM, HDIM), BF16),
        ],
        in_specs=[VMEM] * 2,
        out_specs=[VMEM] * 4,
        compiler_params=pltpu.CompilerParams(vmem_limit_bytes=12 * 2**20),
        cost_estimate=pl.CostEstimate(
            flops=2 * CHIP * 2 * HDIM * HDIM, bytes_accessed=5 * 2**20, transcendentals=CHIP * 512
        ),
    )(mine, other)


def local_kernel(mine, other, key, value, query, inside):
    causal = lax.broadcasted_iota(jnp.int32, (SPAN, SPAN), 0) >= lax.broadcasted_iota(
        jnp.int32, (SPAN, SPAN), 1
    )
    for b in range(CHIP // SPAN):
        for h in range(2):
            at = (slice(b * SPAN, (b + 1) * SPAN), slice(h * HDIM, (h + 1) * HDIM))
            q = silu(mine[at] + other[at].astype(F32)).astype(BF16)
            query[at] = q
            scores = lax.dot_general(
                q, key[at], (((1,), (1,)), ((), ())), preferred_element_type=F32
            )
            scores = jnp.where(causal, scores, 0.0).astype(BF16)
            inside[at] = jnp.dot(scores, value[at], preferred_element_type=F32)


def local_part(mine, other, key, value):
    return pl.pallas_call(
        local_kernel,
        out_shape=[
            jax.ShapeDtypeStruct((CHIP, HALF), BF16),
            jax.ShapeDtypeStruct((CHIP, HALF), F32),
        ],
        in_specs=[VMEM] * 4,
        out_specs=[VMEM] * 2,
        compiler_params=pltpu.CompilerParams(vmem_limit_bytes=12 * 2**20),
        cost_estimate=pl.CostEstimate(
            flops=8 * CHIP * SPAN * HDIM, bytes_accessed=5 * 2**20, transcendentals=CHIP * HALF
        ),
    )(mine, other, key, value)


def finish_kernel(mine, info, query, inside, within, got_0, got_1, got_2, got_3, gain, out):
    core = info[0]
    first = core if mine else 1 - core
    for h in range(2):
        cols = slice(h * HDIM, (h + 1) * HDIM)
        gain_here = gain[:, pl.ds(pl.multiple_of(core * HALF + h * HDIM, HDIM), HDIM)]
        earlier = jnp.zeros((HDIM, HDIM), F32)
        for step, got in enumerate((got_0, got_1, got_2, got_3)):
            earlier = earlier + jnp.where(info[1 + step] > 0, got[h].astype(F32), 0.0)
        for b in range(SLAB // SPAN):
            at = pl.ds(pl.multiple_of(first * SLAB + b * SPAN, SPAN), SPAN)
            state = (earlier + within[first * (SLAB // SPAN) + b, h]).astype(BF16)
            attended = inside[at, cols] + jnp.dot(
                query[at, cols], state, preferred_element_type=F32
            )
            scale = lax.rsqrt(jnp.mean(attended * attended, axis=-1, keepdims=True) + 1e-06)
            out[b * SPAN : (b + 1) * SPAN, cols] = (attended * scale * gain_here).astype(BF16)


def finish(mine, *args):
    return pl.pallas_call(
        functools.partial(finish_kernel, mine),
        out_shape=jax.ShapeDtypeStruct((SLAB, HALF), BF16),
        in_specs=[SMEM] + [VMEM] * 8,
        out_specs=VMEM,
        compiler_params=pltpu.CompilerParams(vmem_limit_bytes=12 * 2**20),
        cost_estimate=pl.CostEstimate(
            flops=4 * SLAB * HDIM * HDIM, bytes_accessed=2 * 2**20, transcendentals=0
        ),
    )(*args)


def after(value, *others):
    return lax.optimization_barrier((value, others))[0]


def pace_kernel(piece, out):
    pass


def pace(piece):
    return pl.pallas_call(
        pace_kernel,
        out_shape=jax.ShapeDtypeStruct(piece.shape, piece.dtype),
        in_specs=[ANY],
        out_specs=ANY,
        input_output_aliases={0: 0},
        compiler_params=pltpu.CompilerParams(vmem_limit_bytes=2**20),
        cost_estimate=pl.CostEstimate(flops=2250000000, bytes_accessed=0, transcendentals=0),
    )(piece)


def gather(tokens, weights, core):
    even = jnp.concatenate([tokens[:, :ROWS], tokens[:, 2 * ROWS : 3 * ROWS]], axis=1)
    odd = jnp.concatenate([tokens[:, ROWS : 2 * ROWS], tokens[:, 3 * ROWS :]], axis=1)
    own = jnp.where(core == 0, even, odd)
    theirs = lax.ppermute(jnp.where(core == 0, odd, even), "seq", SWAP)
    ring = ring_pairs()

    def pass_on(piece):
        return lax.ppermute(piece, ("seq", "head"), ring)

    first, second = [own], [theirs]
    for k in range(1, Z):
        for stream in (first, second):
            piece = stream[-1]
            stream.append(pace(pass_on(piece)))
    streams = list(weights)
    got = [None, None]
    for step in range(4):
        if step:
            got = lax.optimization_barrier(tuple(got))
            streams = [jnp.concatenate(pair, axis=0) for pair in zip(streams, got)]
        got = [lax.ppermute(streams[j], "seq", cube_pairs(j, step)) for j in range(2)]
    blocks = [[streams[j], got[j]] for j in range(2)]
    pieces = zip(first, second)
    return [p for pair in pieces for p in pair], blocks


def local(tokens, w_query, w_key, w_value, gain):
    index = (lax.axis_index("seq") * Z + lax.axis_index("head")).astype(jnp.uint32)
    core = (lax.axis_index("seq").astype(jnp.uint32)) % C
    tokens, index, core = lax.optimization_barrier((tokens, index, core))
    table = jnp.asarray(place_table())
    info = lax.dynamic_slice(table, (index, jnp.uint32(0)), (1, table.shape[1]))[0]
    low, high = (
        jnp.concatenate([w[:, j * HALF : (j + 1) * HALF] for w in (w_key, w_value, w_query)], axis=1)
        for j in range(2)
    )
    halves = [jnp.where(core == 0, high, low), jnp.where(core == 0, low, high)]
    pieces, blocks = gather(tokens, halves, core)

    kv_theirs = product(info, pieces, blocks, 0, 0, 2 * HALF)
    kv_got = lax.ppermute(kv_theirs, "seq", SWAP)
    kv_mine = product(info, pieces, blocks, 1, 0, 2 * HALF)
    key, value, within, total = pair_states(kv_mine, kv_got)

    q_theirs = product(after(info, total), pieces, blocks, 0, 2 * HALF, 3 * HALF)
    q_got = lax.ppermute(q_theirs, "seq", SWAP)
    q_mine = product(after(info, total), pieces, blocks, 1, 2 * HALF, 3 * HALF)
    got, group = [], total
    for step, dim in enumerate((0, 2, 1, 3)):
        if got:
            group = (group.astype(F32) + got[-1].astype(F32)).astype(BF16)
        if step == 1:
            group = after(group, q_theirs)
        if step == 3:
            group = after(group, q_mine)
        got.append(lax.ppermute(group, "seq", exchange_pairs(dim)))
    query, inside = local_part(q_mine, q_got, key, value)

    last = (info, query, inside, within, *got, gain.reshape(1, 2 * HALF))
    out_got = lax.ppermute(finish(False, *last), "seq", SWAP)
    out_mine = finish(True, *last)
    return jnp.concatenate(
        [jnp.where(core == 0, out_mine, out_got), jnp.where(core == 0, out_got, out_mine)], axis=1
    )


def solution(mesh):
    in_specs = (P("seq", "head"), P("seq", "head"), P("seq", "head"), P("seq", "head"), P("head"))
    out_specs = P("seq", "head")
    return jax.shard_map(local, mesh=mesh, in_specs=in_specs, out_specs=out_specs, check_vma=False)
```

```python
import functools

import jax
import jax.numpy as jnp
import numpy as np
from jax import lax
from jax.experimental import pallas as pl
from jax.experimental.pallas import tpu as pltpu
from jax.sharding import PartitionSpec as P

HDIM = 128
SPAN = 256
Y, X, C, Z = 4, 4, 2, 8
ROWS = 192
PIECE = 2 * ROWS
SLAB = 512
CHIP = C * SLAB
HALF = 256
PLACES = 5
BLOCKS = 2
F32, BF16 = jnp.float32, jnp.bfloat16
DIMS = (
    lambda y, x: (y, x ^ 1),
    lambda y, x: (y ^ 1, x),
    lambda y, x: (y, x ^ 3),
    lambda y, x: (y ^ 3, x),
)
ANY = pl.BlockSpec(memory_space=pl.ANY)
VMEM = pl.BlockSpec(memory_space=pltpu.VMEM)
SMEM = pl.BlockSpec(memory_space=pltpu.SMEM)


def seq_of(y, x, c):
    return (y * X + x) * C + c


def chips():
    return [(y, x) for y in range(Y) for x in range(X)]


def dim_of(stream, core, step):
    return (2 * stream + core + step) % 4


def cube_pairs(stream, step):
    return [
        (seq_of(y, x, c), seq_of(*DIMS[dim_of(stream, c, step)](y, x), c))
        for y, x in chips()
        for c in range(C)
    ]


def ring_pairs():
    return [
        (s * Z + z, s * Z + (z + (1 if s % C == 0 else -1)) % Z)
        for s in range(Y * X * C)
        for z in range(Z)
    ]


SWAP = [(s, s ^ 1) for s in range(Y * X * C)]


def exchange_pairs(dim):
    return [(seq_of(y, x, c), seq_of(*DIMS[dim](y, x), c)) for y, x in chips() for c in range(C)]


def place_table():
    table = np.zeros((Y * X * C, Z, PLACES + 4 * Z), np.int32)
    for y, x in chips():
        for c in range(C):
            for z in range(Z):
                places = []
                for stream in range(2):
                    for k in range(Z):
                        for e in range(2):
                            source = 2 * ((z - k if c == 0 else z + k) % Z) + e
                            dx, dy = (source % X) ^ x, (source // X) ^ y
                            bits = (
                                (dx & 1) ^ (dx >> 1),
                                (dy & 1) ^ (dy >> 1),
                                dx >> 1,
                                dy >> 1,
                            )
                            places.append(
                                sum(bits[dim_of(stream, c, step)] << step for step in range(4))
                            )
                after_partner = [x & 1, x >> 1, y & 1, y >> 1]
                table[seq_of(y, x, c), z] = [c] + after_partner + places
    return table.reshape(Y * X * C * Z, PLACES + 4 * Z)


def silu(u):
    return u / (1.0 + jnp.exp(-u))


def product_kernel(mine, low, high, info, *refs):
    tokens, weights, (out, piled) = refs[: 2 * Z], refs[2 * Z : 2 * Z + BLOCKS], refs[-2:]
    core = info[0]
    for slab in range(2):
        first = pl.multiple_of(SLAB * (core if slab == 0 else 1 - core), SLAB)
        total = None
        for k in range(0, Z, 2):
            deep = slice(k * PIECE, (k + 2) * PIECE)
            if slab == 0:
                for at in range(2 * k, 2 * k + 4):
                    place = info[PLACES + mine * 2 * Z + at]
                    row = pl.ds(pl.multiple_of((place % 8) * ROWS, ROWS), ROWS)
                    one, two = (w[row, low:high] for w in weights)
                    piled[at * ROWS : (at + 1) * ROWS] = jnp.where(place < 8, one, two)
            piece = jnp.concatenate(
                [tokens[2 * k + slab][...], tokens[2 * k + 2 + slab][...]], axis=1
            )
            some = jnp.dot(piece, piled[deep], preferred_element_type=F32)
            total = some if total is None else total + some
        out[pl.ds(first, SLAB), :] = total.astype(out.dtype)


def product(info, tokens, blocks, mine, low, high):
    return pl.pallas_call(
        functools.partial(product_kernel, mine, low, high),
        out_shape=jax.ShapeDtypeStruct((CHIP, high - low), F32 if mine else BF16),
        in_specs=[SMEM] + [VMEM] * (2 * Z + BLOCKS),
        out_specs=VMEM,
        scratch_shapes=[pltpu.VMEM((Z * PIECE, high - low), BF16)],
        compiler_params=pltpu.CompilerParams(vmem_limit_bytes=20 * 2**20),
        cost_estimate=pl.CostEstimate(
            flops=2 * CHIP * Z * PIECE * (high - low), bytes_accessed=2**20, transcendentals=0
        ),
    )(info, *tokens, *blocks[mine])


def pairs_kernel(mine, other, key, value, within, total):
    for h in range(2):
        running = jnp.zeros((HDIM, HDIM), F32)
        for b in range(CHIP // SPAN):
            rows = slice(b * SPAN, (b + 1) * SPAN)
            got = []
            for at, out in ((0, key), (HALF, value)):
                cols = slice(at + h * HDIM, at + (h + 1) * HDIM)
                u = mine[rows, cols] + other[rows, cols].astype(F32)
                got.append(silu(u).astype(BF16))
                out[rows, h * HDIM : (h + 1) * HDIM] = got[-1]
            within[b, h] = running
            running = running + lax.dot_general(
                *got, (((0,), (0,)), ((), ())), preferred_element_type=F32
            )
        total[h] = running.astype(BF16)


def pair_states(mine, other):
    return pl.pallas_call(
        pairs_kernel,
        out_shape=[
            jax.ShapeDtypeStruct((CHIP, HALF), BF16),
            jax.ShapeDtypeStruct((CHIP, HALF), BF16),
            jax.ShapeDtypeStruct((CHIP // SPAN, 2, HDIM, HDIM), F32),
            jax.ShapeDtypeStruct((2, HDIM, HDIM), BF16),
        ],
        in_specs=[VMEM] * 2,
        out_specs=[VMEM] * 4,
        compiler_params=pltpu.CompilerParams(vmem_limit_bytes=12 * 2**20),
        cost_estimate=pl.CostEstimate(
            flops=2 * CHIP * 2 * HDIM * HDIM, bytes_accessed=5 * 2**20, transcendentals=CHIP * 512
        ),
    )(mine, other)


def local_kernel(mine, other, key, value, query, inside):
    causal = lax.broadcasted_iota(jnp.int32, (SPAN, SPAN), 0) >= lax.broadcasted_iota(
        jnp.int32, (SPAN, SPAN), 1
    )
    for b in range(CHIP // SPAN):
        for h in range(2):
            at = (slice(b * SPAN, (b + 1) * SPAN), slice(h * HDIM, (h + 1) * HDIM))
            q = silu(mine[at] + other[at].astype(F32)).astype(BF16)
            query[at] = q
            scores = lax.dot_general(
                q, key[at], (((1,), (1,)), ((), ())), preferred_element_type=F32
            )
            scores = jnp.where(causal, scores, 0.0).astype(BF16)
            inside[at] = jnp.dot(scores, value[at], preferred_element_type=F32)


def local_part(mine, other, key, value):
    return pl.pallas_call(
        local_kernel,
        out_shape=[
            jax.ShapeDtypeStruct((CHIP, HALF), BF16),
            jax.ShapeDtypeStruct((CHIP, HALF), F32),
        ],
        in_specs=[VMEM] * 4,
        out_specs=[VMEM] * 2,
        compiler_params=pltpu.CompilerParams(vmem_limit_bytes=12 * 2**20),
        cost_estimate=pl.CostEstimate(
            flops=8 * CHIP * SPAN * HDIM, bytes_accessed=5 * 2**20, transcendentals=CHIP * HALF
        ),
    )(mine, other, key, value)


def finish_kernel(mine, info, query, inside, within, got_0, got_1, got_2, got_3, gain, out):
    core = info[0]
    first = core if mine else 1 - core
    for h in range(2):
        cols = slice(h * HDIM, (h + 1) * HDIM)
        gain_here = gain[:, pl.ds(pl.multiple_of(core * HALF + h * HDIM, HDIM), HDIM)]
        earlier = jnp.zeros((HDIM, HDIM), F32)
        for step, got in enumerate((got_0, got_1, got_2, got_3)):
            earlier = earlier + jnp.where(info[1 + step] > 0, got[h].astype(F32), 0.0)
        for b in range(SLAB // SPAN):
            at = pl.ds(pl.multiple_of(first * SLAB + b * SPAN, SPAN), SPAN)
            state = (earlier + within[first * (SLAB // SPAN) + b, h]).astype(BF16)
            attended = inside[at, cols] + jnp.dot(
                query[at, cols], state, preferred_element_type=F32
            )
            scale = lax.rsqrt(jnp.mean(attended * attended, axis=-1, keepdims=True) + 1e-06)
            out[b * SPAN : (b + 1) * SPAN, cols] = (attended * scale * gain_here).astype(BF16)


def finish(mine, *args):
    return pl.pallas_call(
        functools.partial(finish_kernel, mine),
        out_shape=jax.ShapeDtypeStruct((SLAB, HALF), BF16),
        in_specs=[SMEM] + [VMEM] * 8,
        out_specs=VMEM,
        compiler_params=pltpu.CompilerParams(vmem_limit_bytes=12 * 2**20),
        cost_estimate=pl.CostEstimate(
            flops=4 * SLAB * HDIM * HDIM, bytes_accessed=2 * 2**20, transcendentals=0
        ),
    )(*args)


def after(value, *others):
    return lax.optimization_barrier((value, others))[0]


def pace_kernel(piece, out):
    pass


def pace(piece):
    return pl.pallas_call(
        pace_kernel,
        out_shape=jax.ShapeDtypeStruct(piece.shape, piece.dtype),
        in_specs=[ANY],
        out_specs=ANY,
        input_output_aliases={0: 0},
        compiler_params=pltpu.CompilerParams(vmem_limit_bytes=2**20),
        cost_estimate=pl.CostEstimate(flops=2500000000, bytes_accessed=0, transcendentals=0),
    )(piece)


def gather(tokens, weights, core):
    even = jnp.concatenate([tokens[:, :ROWS], tokens[:, 2 * ROWS : 3 * ROWS]], axis=1)
    odd = jnp.concatenate([tokens[:, ROWS : 2 * ROWS], tokens[:, 3 * ROWS :]], axis=1)
    own = jnp.where(core == 0, even, odd)
    theirs = lax.ppermute(jnp.where(core == 0, odd, even), "seq", SWAP)
    ring = ring_pairs()

    def pass_on(piece):
        return lax.ppermute(piece, ("seq", "head"), ring)

    first, second = [own], [theirs]
    for k in range(1, Z):
        for stream in (first, second):
            piece = stream[-1]
            stream.append(pace(pass_on(piece)))
    streams = list(weights)
    got = [None, None]
    for step in range(4):
        if step:
            streams = [jnp.concatenate(pair, axis=0) for pair in zip(streams, got)]
        got = [lax.ppermute(streams[j], "seq", cube_pairs(j, step)) for j in range(2)]
    blocks = [[streams[j], got[j]] for j in range(2)]
    pieces = zip(first, second)
    return [p for pair in pieces for p in pair], blocks


def local(tokens, w_query, w_key, w_value, gain):
    index = (lax.axis_index("seq") * Z + lax.axis_index("head")).astype(jnp.uint32)
    core = (lax.axis_index("seq").astype(jnp.uint32)) % C
    tokens, index, core = lax.optimization_barrier((tokens, index, core))
    table = jnp.asarray(place_table())
    info = lax.dynamic_slice(table, (index, jnp.uint32(0)), (1, table.shape[1]))[0]
    low, high = (
        jnp.concatenate([w[:, j * HALF : (j + 1) * HALF] for w in (w_key, w_value, w_query)], axis=1)
        for j in range(2)
    )
    halves = [jnp.where(core == 0, high, low), jnp.where(core == 0, low, high)]
    pieces, blocks = gather(tokens, halves, core)

    kv_theirs = product(after(info, blocks[1][1]), pieces, blocks, 0, 0, 2 * HALF)
    kv_got = lax.ppermute(kv_theirs, "seq", SWAP)
    kv_mine = product(info, pieces, blocks, 1, 0, 2 * HALF)
    key, value, within, total = pair_states(kv_mine, kv_got)

    q_theirs = product(after(info, total), pieces, blocks, 0, 2 * HALF, 3 * HALF)
    q_got = lax.ppermute(q_theirs, "seq", SWAP)
    q_mine = product(after(info, total), pieces, blocks, 1, 2 * HALF, 3 * HALF)
    got, group = [], total
    for step, dim in enumerate((0, 2, 1, 3)):
        if got:
            group = (group.astype(F32) + got[-1].astype(F32)).astype(BF16)
        if step == 1:
            group = after(group, q_theirs)
        if step == 3:
            group = after(group, q_mine)
        got.append(lax.ppermute(group, "seq", exchange_pairs(dim)))
    query, inside = local_part(q_mine, q_got, key, value)

    last = (info, query, inside, within, *got, gain.reshape(1, 2 * HALF))
    out_got = lax.ppermute(finish(False, *last), "seq", SWAP)
    out_mine = finish(True, *last)
    return jnp.concatenate(
        [jnp.where(core == 0, out_mine, out_got), jnp.where(core == 0, out_got, out_mine)], axis=1
    )


def solution(mesh):
    in_specs = (P("seq", "head"), P("seq", "head"), P("seq", "head"), P("seq", "head"), P("head"))
    out_specs = P("seq", "head")
    return jax.shard_map(local, mesh=mesh, in_specs=in_specs, out_specs=out_specs, check_vma=False)
```

```python
import functools

import jax
import jax.numpy as jnp
import numpy as np
from jax import lax
from jax.experimental import pallas as pl
from jax.experimental.pallas import tpu as pltpu
from jax.sharding import PartitionSpec as P

HDIM = 128
SPAN = 256
Y, X, C, Z = 4, 4, 2, 8
ROWS = 192
PIECE = 2 * ROWS
SLAB = 512
CHIP = C * SLAB
HALF = 256
PLACES = 5
BLOCKS = 2
F32, BF16 = jnp.float32, jnp.bfloat16
DIMS = (
    lambda y, x: (y, x ^ 1),
    lambda y, x: (y ^ 1, x),
    lambda y, x: (y, x ^ 3),
    lambda y, x: (y ^ 3, x),
)
ANY = pl.BlockSpec(memory_space=pl.ANY)
VMEM = pl.BlockSpec(memory_space=pltpu.VMEM)
SMEM = pl.BlockSpec(memory_space=pltpu.SMEM)


def seq_of(y, x, c):
    return (y * X + x) * C + c


def chips():
    return [(y, x) for y in range(Y) for x in range(X)]


def dim_of(stream, core, step):
    return (2 * stream + core + step) % 4


def cube_pairs(stream, step):
    return [
        (seq_of(y, x, c), seq_of(*DIMS[dim_of(stream, c, step)](y, x), c))
        for y, x in chips()
        for c in range(C)
    ]


def ring_pairs():
    return [
        (s * Z + z, s * Z + (z + (1 if s % C == 0 else -1)) % Z)
        for s in range(Y * X * C)
        for z in range(Z)
    ]


SWAP = [(s, s ^ 1) for s in range(Y * X * C)]


def exchange_pairs(dim):
    return [(seq_of(y, x, c), seq_of(*DIMS[dim](y, x), c)) for y, x in chips() for c in range(C)]


def place_table():
    table = np.zeros((Y * X * C, Z, PLACES + 4 * Z), np.int32)
    for y, x in chips():
        for c in range(C):
            for z in range(Z):
                places = []
                for stream in range(2):
                    for k in range(Z):
                        for e in range(2):
                            source = 2 * ((z - k if c == 0 else z + k) % Z) + e
                            dx, dy = (source % X) ^ x, (source // X) ^ y
                            bits = (
                                (dx & 1) ^ (dx >> 1),
                                (dy & 1) ^ (dy >> 1),
                                dx >> 1,
                                dy >> 1,
                            )
                            places.append(
                                sum(bits[dim_of(stream, c, step)] << step for step in range(4))
                            )
                after_partner = [x & 1, x >> 1, y & 1, y >> 1]
                table[seq_of(y, x, c), z] = [c] + after_partner + places
    return table.reshape(Y * X * C * Z, PLACES + 4 * Z)


def silu(u):
    return u / (1.0 + jnp.exp(-u))


def product_kernel(mine, info, *refs):
    tokens, weights, (out, piled) = refs[: 2 * Z], refs[2 * Z : 2 * Z + BLOCKS], refs[-2:]
    core = info[0]
    for slab in range(2):
        first = pl.multiple_of(SLAB * (core if slab == 0 else 1 - core), SLAB)
        total = None
        for k in range(0, Z, 2):
            deep = slice(k * PIECE, (k + 2) * PIECE)
            if slab == 0:
                for at in range(2 * k, 2 * k + 4):
                    place = info[PLACES + mine * 2 * Z + at]
                    row = pl.ds(pl.multiple_of((place % 8) * ROWS, ROWS), ROWS)
                    one, two = (w[row, :] for w in weights)
                    piled[at * ROWS : (at + 1) * ROWS] = jnp.where(place < 8, one, two)
            piece = jnp.concatenate(
                [tokens[2 * k + slab][...], tokens[2 * k + 2 + slab][...]], axis=1
            )
            some = jnp.dot(piece, piled[deep], preferred_element_type=F32)
            total = some if total is None else total + some
        out[pl.ds(first, SLAB), :] = total.astype(out.dtype)


def product(info, tokens, blocks, mine):
    width = blocks[mine][0].shape[1]
    return pl.pallas_call(
        functools.partial(product_kernel, mine),
        out_shape=jax.ShapeDtypeStruct((CHIP, width), F32 if mine else BF16),
        in_specs=[SMEM] + [VMEM] * (2 * Z + BLOCKS),
        out_specs=VMEM,
        scratch_shapes=[pltpu.VMEM((Z * PIECE, width), BF16)],
        compiler_params=pltpu.CompilerParams(vmem_limit_bytes=20 * 2**20),
        cost_estimate=pl.CostEstimate(
            flops=2 * CHIP * Z * PIECE * width, bytes_accessed=2**20, transcendentals=0
        ),
    )(info, *tokens, *blocks[mine])


def pairs_kernel(mine, other, key, value, within, total):
    for h in range(2):
        running = jnp.zeros((HDIM, HDIM), F32)
        for b in range(CHIP // SPAN):
            rows = slice(b * SPAN, (b + 1) * SPAN)
            got = []
            for at, out in ((0, key), (HALF, value)):
                cols = slice(at + h * HDIM, at + (h + 1) * HDIM)
                u = mine[rows, cols] + other[rows, cols].astype(F32)
                got.append(silu(u).astype(BF16))
                out[rows, h * HDIM : (h + 1) * HDIM] = got[-1]
            within[b, h] = running
            running = running + lax.dot_general(
                *got, (((0,), (0,)), ((), ())), preferred_element_type=F32
            )
        total[h] = running.astype(BF16)


def pair_states(mine, other):
    return pl.pallas_call(
        pairs_kernel,
        out_shape=[
            jax.ShapeDtypeStruct((CHIP, HALF), BF16),
            jax.ShapeDtypeStruct((CHIP, HALF), BF16),
            jax.ShapeDtypeStruct((CHIP // SPAN, 2, HDIM, HDIM), F32),
            jax.ShapeDtypeStruct((2, HDIM, HDIM), BF16),
        ],
        in_specs=[VMEM] * 2,
        out_specs=[VMEM] * 4,
        compiler_params=pltpu.CompilerParams(vmem_limit_bytes=12 * 2**20),
        cost_estimate=pl.CostEstimate(
            flops=2 * CHIP * 2 * HDIM * HDIM, bytes_accessed=5 * 2**20, transcendentals=CHIP * 512
        ),
    )(mine, other)


def local_kernel(mine, other, key, value, query, inside):
    causal = lax.broadcasted_iota(jnp.int32, (SPAN, SPAN), 0) >= lax.broadcasted_iota(
        jnp.int32, (SPAN, SPAN), 1
    )
    for b in range(CHIP // SPAN):
        for h in range(2):
            at = (slice(b * SPAN, (b + 1) * SPAN), slice(h * HDIM, (h + 1) * HDIM))
            q = silu(mine[at] + other[at].astype(F32)).astype(BF16)
            query[at] = q
            scores = lax.dot_general(
                q, key[at], (((1,), (1,)), ((), ())), preferred_element_type=F32
            )
            scores = jnp.where(causal, scores, 0.0).astype(BF16)
            inside[at] = jnp.dot(scores, value[at], preferred_element_type=F32)


def local_part(mine, other, key, value):
    return pl.pallas_call(
        local_kernel,
        out_shape=[
            jax.ShapeDtypeStruct((CHIP, HALF), BF16),
            jax.ShapeDtypeStruct((CHIP, HALF), F32),
        ],
        in_specs=[VMEM] * 4,
        out_specs=[VMEM] * 2,
        compiler_params=pltpu.CompilerParams(vmem_limit_bytes=12 * 2**20),
        cost_estimate=pl.CostEstimate(
            flops=8 * CHIP * SPAN * HDIM, bytes_accessed=5 * 2**20, transcendentals=CHIP * HALF
        ),
    )(mine, other, key, value)


def finish_kernel(mine, info, query, inside, within, got_0, got_1, got_2, got_3, gain, out):
    core = info[0]
    first = core if mine else 1 - core
    for h in range(2):
        cols = slice(h * HDIM, (h + 1) * HDIM)
        gain_here = gain[:, pl.ds(pl.multiple_of(core * HALF + h * HDIM, HDIM), HDIM)]
        earlier = jnp.zeros((HDIM, HDIM), F32)
        for step, got in enumerate((got_0, got_1, got_2, got_3)):
            earlier = earlier + jnp.where(info[1 + step] > 0, got[h].astype(F32), 0.0)
        for b in range(SLAB // SPAN):
            at = pl.ds(pl.multiple_of(first * SLAB + b * SPAN, SPAN), SPAN)
            state = (earlier + within[first * (SLAB // SPAN) + b, h]).astype(BF16)
            attended = inside[at, cols] + jnp.dot(
                query[at, cols], state, preferred_element_type=F32
            )
            scale = lax.rsqrt(jnp.mean(attended * attended, axis=-1, keepdims=True) + 1e-06)
            out[b * SPAN : (b + 1) * SPAN, cols] = (attended * scale * gain_here).astype(BF16)


def finish(mine, *args):
    return pl.pallas_call(
        functools.partial(finish_kernel, mine),
        out_shape=jax.ShapeDtypeStruct((SLAB, HALF), BF16),
        in_specs=[SMEM] + [VMEM] * 8,
        out_specs=VMEM,
        compiler_params=pltpu.CompilerParams(vmem_limit_bytes=12 * 2**20),
        cost_estimate=pl.CostEstimate(
            flops=4 * SLAB * HDIM * HDIM, bytes_accessed=2 * 2**20, transcendentals=0
        ),
    )(*args)


def after(value, *others):
    return lax.optimization_barrier((value, others))[0]


def pace_kernel(piece, out):
    pass


def pace(piece):
    return pl.pallas_call(
        pace_kernel,
        out_shape=jax.ShapeDtypeStruct(piece.shape, piece.dtype),
        in_specs=[ANY],
        out_specs=ANY,
        input_output_aliases={0: 0},
        compiler_params=pltpu.CompilerParams(vmem_limit_bytes=2**20),
        cost_estimate=pl.CostEstimate(flops=2500000000, bytes_accessed=0, transcendentals=0),
    )(piece)


def gather(tokens, weights, core):
    even = jnp.concatenate([tokens[:, :ROWS], tokens[:, 2 * ROWS : 3 * ROWS]], axis=1)
    odd = jnp.concatenate([tokens[:, ROWS : 2 * ROWS], tokens[:, 3 * ROWS :]], axis=1)
    own = jnp.where(core == 0, even, odd)
    theirs = lax.ppermute(jnp.where(core == 0, odd, even), "seq", SWAP)
    ring = ring_pairs()

    def pass_on(piece):
        return lax.ppermute(piece, ("seq", "head"), ring)

    first, second = [own], [theirs]
    for k in range(1, Z):
        for stream in (first, second):
            piece = stream[-1]
            stream.append(pace(pass_on(piece)))
    streams = list(weights)
    for step in range(3):
        got = [lax.ppermute(streams[j], "seq", cube_pairs(j, step)) for j in range(2)]
        pairs = list(zip(streams, got))
        if step < 2:
            streams = [jnp.concatenate(pair, axis=0) for pair in pairs]
    blocks = []
    for low, high in ((0, 2 * HALF), (2 * HALF, 3 * HALF)):
        near = [jnp.concatenate([part[:, low:high] for part in pair], axis=0) for pair in pairs]
        if low:
            near = [after(part, second[-1]) for part in near]
        blocks.append([[near[j], lax.ppermute(near[j], "seq", cube_pairs(j, 3))] for j in range(2)])
    pieces = zip(first, second)
    return [p for pair in pieces for p in pair], blocks


def local(tokens, w_query, w_key, w_value, gain):
    index = (lax.axis_index("seq") * Z + lax.axis_index("head")).astype(jnp.uint32)
    core = (lax.axis_index("seq").astype(jnp.uint32)) % C
    tokens, index, core = lax.optimization_barrier((tokens, index, core))
    table = jnp.asarray(place_table())
    info = lax.dynamic_slice(table, (index, jnp.uint32(0)), (1, table.shape[1]))[0]
    low, high = (
        jnp.concatenate([w[:, j * HALF : (j + 1) * HALF] for w in (w_key, w_value, w_query)], axis=1)
        for j in range(2)
    )
    halves = [jnp.where(core == 0, high, low), jnp.where(core == 0, low, high)]
    pieces, (kv_blocks, q_blocks) = gather(tokens, halves, core)

    kv_theirs = product(after(info, kv_blocks[1][1]), pieces, kv_blocks, 0)
    kv_got = lax.ppermute(kv_theirs, "seq", SWAP)
    kv_mine = product(info, pieces, kv_blocks, 1)
    key, value, within, total = pair_states(kv_mine, kv_got)

    q_theirs = product(after(info, total), pieces, q_blocks, 0)
    q_got = lax.ppermute(q_theirs, "seq", SWAP)
    q_mine = product(after(info, total), pieces, q_blocks, 1)
    got, group = [], total
    for step, dim in enumerate((0, 2, 1, 3)):
        if got:
            group = (group.astype(F32) + got[-1].astype(F32)).astype(BF16)
        if step == 1:
            group = after(group, q_theirs)
        if step == 3:
            group = after(group, q_mine)
        got.append(lax.ppermute(group, "seq", exchange_pairs(dim)))
    query, inside = local_part(q_mine, q_got, key, value)

    last = (info, query, inside, within, *got, gain.reshape(1, 2 * HALF))
    out_got = lax.ppermute(finish(False, *last), "seq", SWAP)
    out_mine = finish(True, *last)
    return jnp.concatenate(
        [jnp.where(core == 0, out_mine, out_got), jnp.where(core == 0, out_got, out_mine)], axis=1
    )


def solution(mesh):
    in_specs = (P("seq", "head"), P("seq", "head"), P("seq", "head"), P("seq", "head"), P("head"))
    out_specs = P("seq", "head")
    return jax.shard_map(local, mesh=mesh, in_specs=in_specs, out_specs=out_specs, check_vma=False)
```

```python
import functools

import jax
import jax.numpy as jnp
import numpy as np
from jax import lax
from jax.experimental import pallas as pl
from jax.experimental.pallas import tpu as pltpu
from jax.sharding import PartitionSpec as P

HDIM = 128
SPAN = 256
Y, X, C, Z = 4, 4, 2, 8
ROWS = 192
PIECE = 2 * ROWS
SLAB = 512
CHIP = C * SLAB
HALF = 256
PLACES = 5
BLOCKS = 2
F32, BF16 = jnp.float32, jnp.bfloat16
DIMS = (
    lambda y, x: (y, x ^ 1),
    lambda y, x: (y ^ 1, x),
    lambda y, x: (y, x ^ 3),
    lambda y, x: (y ^ 3, x),
)
ANY = pl.BlockSpec(memory_space=pl.ANY)
VMEM = pl.BlockSpec(memory_space=pltpu.VMEM)
SMEM = pl.BlockSpec(memory_space=pltpu.SMEM)


def seq_of(y, x, c):
    return (y * X + x) * C + c


def chips():
    return [(y, x) for y in range(Y) for x in range(X)]


def dim_of(stream, core, step):
    return (2 * stream + core + step) % 4


def cube_pairs(stream, step):
    return [
        (seq_of(y, x, c), seq_of(*DIMS[dim_of(stream, c, step)](y, x), c))
        for y, x in chips()
        for c in range(C)
    ]


def ring_pairs():
    return [
        (s * Z + z, s * Z + (z + (1 if s % C == 0 else -1)) % Z)
        for s in range(Y * X * C)
        for z in range(Z)
    ]


SWAP = [(s, s ^ 1) for s in range(Y * X * C)]


def exchange_pairs(dim):
    return [(seq_of(y, x, c), seq_of(*DIMS[dim](y, x), c)) for y, x in chips() for c in range(C)]


def place_table():
    table = np.zeros((Y * X * C, Z, PLACES + 4 * Z), np.int32)
    for y, x in chips():
        for c in range(C):
            for z in range(Z):
                places = []
                for stream in range(2):
                    for k in range(Z):
                        for e in range(2):
                            source = 2 * ((z - k if c == 0 else z + k) % Z) + e
                            dx, dy = (source % X) ^ x, (source // X) ^ y
                            bits = (
                                (dx & 1) ^ (dx >> 1),
                                (dy & 1) ^ (dy >> 1),
                                dx >> 1,
                                dy >> 1,
                            )
                            places.append(
                                sum(bits[dim_of(stream, c, step)] << step for step in range(4))
                            )
                after_partner = [x & 1, x >> 1, y & 1, y >> 1]
                table[seq_of(y, x, c), z] = [c] + after_partner + places
    return table.reshape(Y * X * C * Z, PLACES + 4 * Z)


def silu(u):
    return u / (1.0 + jnp.exp(-u))


def product_kernel(mine, info, *refs):
    tokens, weights, (out, piled) = refs[: 2 * Z], refs[2 * Z : 2 * Z + BLOCKS], refs[-2:]
    core = info[0]
    for slab in range(2):
        first = pl.multiple_of(SLAB * (core if slab == 0 else 1 - core), SLAB)
        total = None
        for k in range(0, Z, 2):
            deep = slice(k * PIECE, (k + 2) * PIECE)
            if slab == 0:
                for at in range(2 * k, 2 * k + 4):
                    place = info[PLACES + mine * 2 * Z + at]
                    row = pl.ds(pl.multiple_of((place % 8) * ROWS, ROWS), ROWS)
                    one, two = (w[row, :] for w in weights)
                    piled[at * ROWS : (at + 1) * ROWS] = jnp.where(place < 8, one, two)
            piece = jnp.concatenate(
                [tokens[2 * k + slab][...], tokens[2 * k + 2 + slab][...]], axis=1
            )
            some = jnp.dot(piece, piled[deep], preferred_element_type=F32)
            total = some if total is None else total + some
        out[pl.ds(first, SLAB), :] = total.astype(out.dtype)


def product(info, tokens, blocks, mine):
    width = blocks[mine][0].shape[1]
    return pl.pallas_call(
        functools.partial(product_kernel, mine),
        out_shape=jax.ShapeDtypeStruct((CHIP, width), F32 if mine else BF16),
        in_specs=[SMEM] + [VMEM] * (2 * Z + BLOCKS),
        out_specs=VMEM,
        scratch_shapes=[pltpu.VMEM((Z * PIECE, width), BF16)],
        compiler_params=pltpu.CompilerParams(vmem_limit_bytes=20 * 2**20),
        cost_estimate=pl.CostEstimate(
            flops=2 * CHIP * Z * PIECE * width, bytes_accessed=2**20, transcendentals=0
        ),
    )(info, *tokens, *blocks[mine])


def pairs_kernel(mine, other, key, value, within, total):
    for h in range(2):
        running = jnp.zeros((HDIM, HDIM), F32)
        for b in range(CHIP // SPAN):
            rows = slice(b * SPAN, (b + 1) * SPAN)
            got = []
            for at, out in ((0, key), (HALF, value)):
                cols = slice(at + h * HDIM, at + (h + 1) * HDIM)
                u = mine[rows, cols] + other[rows, cols].astype(F32)
                got.append(silu(u).astype(BF16))
                out[rows, h * HDIM : (h + 1) * HDIM] = got[-1]
            within[b, h] = running
            running = running + lax.dot_general(
                *got, (((0,), (0,)), ((), ())), preferred_element_type=F32
            )
        total[h] = running.astype(BF16)


def pair_states(mine, other):
    return pl.pallas_call(
        pairs_kernel,
        out_shape=[
            jax.ShapeDtypeStruct((CHIP, HALF), BF16),
            jax.ShapeDtypeStruct((CHIP, HALF), BF16),
            jax.ShapeDtypeStruct((CHIP // SPAN, 2, HDIM, HDIM), F32),
            jax.ShapeDtypeStruct((2, HDIM, HDIM), BF16),
        ],
        in_specs=[VMEM] * 2,
        out_specs=[VMEM] * 4,
        compiler_params=pltpu.CompilerParams(vmem_limit_bytes=12 * 2**20),
        cost_estimate=pl.CostEstimate(
            flops=2 * CHIP * 2 * HDIM * HDIM, bytes_accessed=5 * 2**20, transcendentals=CHIP * 512
        ),
    )(mine, other)


def local_kernel(mine, other, key, value, query, inside):
    causal = lax.broadcasted_iota(jnp.int32, (SPAN, SPAN), 0) >= lax.broadcasted_iota(
        jnp.int32, (SPAN, SPAN), 1
    )
    for b in range(CHIP // SPAN):
        for h in range(2):
            at = (slice(b * SPAN, (b + 1) * SPAN), slice(h * HDIM, (h + 1) * HDIM))
            q = silu(mine[at] + other[at].astype(F32)).astype(BF16)
            query[at] = q
            scores = lax.dot_general(
                q, key[at], (((1,), (1,)), ((), ())), preferred_element_type=F32
            )
            scores = jnp.where(causal, scores, 0.0).astype(BF16)
            inside[at] = jnp.dot(scores, value[at], preferred_element_type=F32)


def local_part(mine, other, key, value):
    return pl.pallas_call(
        local_kernel,
        out_shape=[
            jax.ShapeDtypeStruct((CHIP, HALF), BF16),
            jax.ShapeDtypeStruct((CHIP, HALF), F32),
        ],
        in_specs=[VMEM] * 4,
        out_specs=[VMEM] * 2,
        compiler_params=pltpu.CompilerParams(vmem_limit_bytes=12 * 2**20),
        cost_estimate=pl.CostEstimate(
            flops=8 * CHIP * SPAN * HDIM, bytes_accessed=5 * 2**20, transcendentals=CHIP * HALF
        ),
    )(mine, other, key, value)


def finish_kernel(mine, info, query, inside, within, got_0, got_1, got_2, got_3, gain, out):
    core = info[0]
    first = core if mine else 1 - core
    for h in range(2):
        cols = slice(h * HDIM, (h + 1) * HDIM)
        gain_here = gain[:, pl.ds(pl.multiple_of(core * HALF + h * HDIM, HDIM), HDIM)]
        earlier = jnp.zeros((HDIM, HDIM), F32)
        for step, got in enumerate((got_0, got_1, got_2, got_3)):
            earlier = earlier + jnp.where(info[1 + step] > 0, got[h].astype(F32), 0.0)
        for b in range(SLAB // SPAN):
            at = pl.ds(pl.multiple_of(first * SLAB + b * SPAN, SPAN), SPAN)
            state = (earlier + within[first * (SLAB // SPAN) + b, h]).astype(BF16)
            attended = inside[at, cols] + jnp.dot(
                query[at, cols], state, preferred_element_type=F32
            )
            scale = lax.rsqrt(jnp.mean(attended * attended, axis=-1, keepdims=True) + 1e-06)
            out[b * SPAN : (b + 1) * SPAN, cols] = (attended * scale * gain_here).astype(BF16)


def finish(mine, *args):
    return pl.pallas_call(
        functools.partial(finish_kernel, mine),
        out_shape=jax.ShapeDtypeStruct((SLAB, HALF), BF16),
        in_specs=[SMEM] + [VMEM] * 8,
        out_specs=VMEM,
        compiler_params=pltpu.CompilerParams(vmem_limit_bytes=12 * 2**20),
        cost_estimate=pl.CostEstimate(
            flops=4 * SLAB * HDIM * HDIM, bytes_accessed=2 * 2**20, transcendentals=0
        ),
    )(*args)


def after(value, *others):
    return lax.optimization_barrier((value, others))[0]


def pace_kernel(piece, out):
    pass


def pace(piece):
    return pl.pallas_call(
        pace_kernel,
        out_shape=jax.ShapeDtypeStruct(piece.shape, piece.dtype),
        in_specs=[ANY],
        out_specs=ANY,
        input_output_aliases={0: 0},
        compiler_params=pltpu.CompilerParams(vmem_limit_bytes=2**20),
        cost_estimate=pl.CostEstimate(flops=2500000000, bytes_accessed=0, transcendentals=0),
    )(piece)


def gather(tokens, weights, core):
    even = jnp.concatenate([tokens[:, :ROWS], tokens[:, 2 * ROWS : 3 * ROWS]], axis=1)
    odd = jnp.concatenate([tokens[:, ROWS : 2 * ROWS], tokens[:, 3 * ROWS :]], axis=1)
    own = jnp.where(core == 0, even, odd)
    theirs = lax.ppermute(jnp.where(core == 0, odd, even), "seq", SWAP)
    ring = ring_pairs()

    def pass_on(piece):
        return lax.ppermute(piece, ("seq", "head"), ring)

    first, second = [own], [theirs]
    for k in range(1, Z):
        for stream in (first, second):
            piece = stream[-1]
            stream.append(pace(pass_on(piece)))
    streams = list(weights)
    for step in range(3):
        got = [lax.ppermute(streams[j], "seq", cube_pairs(j, step)) for j in range(2)]
        pairs = list(zip(streams, got))
        if step < 2:
            streams = [jnp.concatenate(pair, axis=0) for pair in pairs]
    blocks = []
    for low, high in ((0, 2 * HALF), (2 * HALF, 3 * HALF)):
        near = [jnp.concatenate([part[:, low:high] for part in pair], axis=0) for pair in pairs]
        if low:
            near = [after(part, first[-1]) for part in near]
        blocks.append([[near[j], lax.ppermute(near[j], "seq", cube_pairs(j, 3))] for j in range(2)])
    pieces = zip(first, second)
    return [p for pair in pieces for p in pair], blocks


def local(tokens, w_query, w_key, w_value, gain):
    index = (lax.axis_index("seq") * Z + lax.axis_index("head")).astype(jnp.uint32)
    core = (lax.axis_index("seq").astype(jnp.uint32)) % C
    tokens, index, core = lax.optimization_barrier((tokens, index, core))
    table = jnp.asarray(place_table())
    info = lax.dynamic_slice(table, (index, jnp.uint32(0)), (1, table.shape[1]))[0]
    low, high = (
        jnp.concatenate([w[:, j * HALF : (j + 1) * HALF] for w in (w_key, w_value, w_query)], axis=1)
        for j in range(2)
    )
    halves = [jnp.where(core == 0, high, low), jnp.where(core == 0, low, high)]
    pieces, (kv_blocks, q_blocks) = gather(tokens, halves, core)

    kv_theirs = product(after(info, kv_blocks[1][1]), pieces, kv_blocks, 0)
    kv_got = lax.ppermute(kv_theirs, "seq", SWAP)
    kv_mine = product(info, pieces, kv_blocks, 1)
    key, value, within, total = pair_states(kv_mine, kv_got)

    q_theirs = product(after(info, total), pieces, q_blocks, 0)
    q_got = lax.ppermute(q_theirs, "seq", SWAP)
    q_mine = product(after(info, total), pieces, q_blocks, 1)
    got, group = [], total
    for step, dim in enumerate((0, 2, 1, 3)):
        if got:
            group = (group.astype(F32) + got[-1].astype(F32)).astype(BF16)
        if step == 2:
            group = after(group, q_theirs)
        if step == 3:
            group = after(group, q_mine)
        got.append(lax.ppermute(group, "seq", exchange_pairs(dim)))
    query, inside = local_part(q_mine, q_got, key, value)

    last = (info, query, inside, within, *got, gain.reshape(1, 2 * HALF))
    out_got = lax.ppermute(finish(False, *last), "seq", SWAP)
    out_mine = finish(True, *last)
    return jnp.concatenate(
        [jnp.where(core == 0, out_mine, out_got), jnp.where(core == 0, out_got, out_mine)], axis=1
    )


def solution(mesh):
    in_specs = (P("seq", "head"), P("seq", "head"), P("seq", "head"), P("seq", "head"), P("head"))
    out_specs = P("seq", "head")
    return jax.shard_map(local, mesh=mesh, in_specs=in_specs, out_specs=out_specs, check_vma=False)
```

```python
import functools

import jax
import jax.numpy as jnp
import numpy as np
from jax import lax
from jax.experimental import pallas as pl
from jax.experimental.pallas import tpu as pltpu
from jax.sharding import PartitionSpec as P

HDIM = 128
SPAN = 256
Y, X, C, Z = 4, 4, 2, 8
ROWS = 192
PIECE = 2 * ROWS
SLAB = 512
CHIP = C * SLAB
HALF = 256
PLACES = 5
BLOCKS = 2
F32, BF16 = jnp.float32, jnp.bfloat16
DIMS = (
    lambda y, x: (y, x ^ 1),
    lambda y, x: (y ^ 1, x),
    lambda y, x: (y, x ^ 3),
    lambda y, x: (y ^ 3, x),
)
ANY = pl.BlockSpec(memory_space=pl.ANY)
VMEM = pl.BlockSpec(memory_space=pltpu.VMEM)
SMEM = pl.BlockSpec(memory_space=pltpu.SMEM)


def seq_of(y, x, c):
    return (y * X + x) * C + c


def chips():
    return [(y, x) for y in range(Y) for x in range(X)]


def dim_of(stream, core, step):
    return (2 * stream + core + step) % 4


def cube_pairs(stream, step):
    return [
        (seq_of(y, x, c), seq_of(*DIMS[dim_of(stream, c, step)](y, x), c))
        for y, x in chips()
        for c in range(C)
    ]


def ring_pairs(stream):
    return [
        (s * Z + z, s * Z + (z + (1 if (s + stream) % 2 == 0 else -1)) % Z)
        for s in range(Y * X * C)
        for z in range(Z)
    ]


SWAP = [(s, s ^ 1) for s in range(Y * X * C)]


def exchange_pairs(dim):
    return [(seq_of(y, x, c), seq_of(*DIMS[dim](y, x), c)) for y, x in chips() for c in range(C)]


def place_table():
    table = np.zeros((Y * X * C, Z, PLACES + 4 * Z), np.int32)
    for y, x in chips():
        for c in range(C):
            for z in range(Z):
                places = []
                for stream in range(2):
                    for k in range(Z):
                        for e in range(2):
                            source = 2 * ((z - k if c == 0 else z + k) % Z) + e
                            dx, dy = (source % X) ^ x, (source // X) ^ y
                            bits = (
                                (dx & 1) ^ (dx >> 1),
                                (dy & 1) ^ (dy >> 1),
                                dx >> 1,
                                dy >> 1,
                            )
                            places.append(
                                sum(bits[dim_of(stream, c, step)] << step for step in range(4))
                            )
                after_partner = [x & 1, x >> 1, y & 1, y >> 1]
                table[seq_of(y, x, c), z] = [c] + after_partner + places
    return table.reshape(Y * X * C * Z, PLACES + 4 * Z)


def silu(u):
    return u / (1.0 + jnp.exp(-u))


def product_kernel(mine, info, *refs):
    tokens, weights, (out, piled) = refs[: 2 * Z], refs[2 * Z : 2 * Z + BLOCKS], refs[-2:]
    core = info[0]
    for slab in range(2):
        first = pl.multiple_of(SLAB * (core if slab == 0 else 1 - core), SLAB)
        total = None
        for k in range(0, Z, 2):
            deep = slice(k * PIECE, (k + 2) * PIECE)
            if slab == 0:
                for at in range(2 * k, 2 * k + 4):
                    place = info[PLACES + mine * 2 * Z + at]
                    row = pl.ds(pl.multiple_of((place % 8) * ROWS, ROWS), ROWS)
                    one, two = (w[row, :] for w in weights)
                    piled[at * ROWS : (at + 1) * ROWS] = jnp.where(place < 8, one, two)
            piece = jnp.concatenate(
                [tokens[2 * k + slab][...], tokens[2 * k + 2 + slab][...]], axis=1
            )
            some = jnp.dot(piece, piled[deep], preferred_element_type=F32)
            total = some if total is None else total + some
        out[pl.ds(first, SLAB), :] = total.astype(out.dtype)


def product(info, tokens, blocks, mine):
    width = blocks[mine][0].shape[1]
    return pl.pallas_call(
        functools.partial(product_kernel, mine),
        out_shape=jax.ShapeDtypeStruct((CHIP, width), F32 if mine else BF16),
        in_specs=[SMEM] + [VMEM] * (2 * Z + BLOCKS),
        out_specs=VMEM,
        scratch_shapes=[pltpu.VMEM((Z * PIECE, width), BF16)],
        compiler_params=pltpu.CompilerParams(vmem_limit_bytes=20 * 2**20),
        cost_estimate=pl.CostEstimate(
            flops=2 * CHIP * Z * PIECE * width, bytes_accessed=2**20, transcendentals=0
        ),
    )(info, *tokens, *blocks[mine])


def pairs_kernel(mine, other, key, value, within, total):
    for h in range(2):
        running = jnp.zeros((HDIM, HDIM), F32)
        for b in range(CHIP // SPAN):
            rows = slice(b * SPAN, (b + 1) * SPAN)
            got = []
            for at, out in ((0, key), (HALF, value)):
                cols = slice(at + h * HDIM, at + (h + 1) * HDIM)
                u = mine[rows, cols] + other[rows, cols].astype(F32)
                got.append(silu(u).astype(BF16))
                out[rows, h * HDIM : (h + 1) * HDIM] = got[-1]
            within[b, h] = running
            running = running + lax.dot_general(
                *got, (((0,), (0,)), ((), ())), preferred_element_type=F32
            )
        total[h] = running.astype(BF16)


def pair_states(mine, other):
    return pl.pallas_call(
        pairs_kernel,
        out_shape=[
            jax.ShapeDtypeStruct((CHIP, HALF), BF16),
            jax.ShapeDtypeStruct((CHIP, HALF), BF16),
            jax.ShapeDtypeStruct((CHIP // SPAN, 2, HDIM, HDIM), F32),
            jax.ShapeDtypeStruct((2, HDIM, HDIM), BF16),
        ],
        in_specs=[VMEM] * 2,
        out_specs=[VMEM] * 4,
        compiler_params=pltpu.CompilerParams(vmem_limit_bytes=12 * 2**20),
        cost_estimate=pl.CostEstimate(
            flops=2 * CHIP * 2 * HDIM * HDIM, bytes_accessed=5 * 2**20, transcendentals=CHIP * 512
        ),
    )(mine, other)


def local_kernel(mine, other, key, value, query, inside):
    causal = lax.broadcasted_iota(jnp.int32, (SPAN, SPAN), 0) >= lax.broadcasted_iota(
        jnp.int32, (SPAN, SPAN), 1
    )
    for b in range(CHIP // SPAN):
        for h in range(2):
            at = (slice(b * SPAN, (b + 1) * SPAN), slice(h * HDIM, (h + 1) * HDIM))
            q = silu(mine[at] + other[at].astype(F32)).astype(BF16)
            query[at] = q
            scores = lax.dot_general(
                q, key[at], (((1,), (1,)), ((), ())), preferred_element_type=F32
            )
            scores = jnp.where(causal, scores, 0.0).astype(BF16)
            inside[at] = jnp.dot(scores, value[at], preferred_element_type=F32)


def local_part(mine, other, key, value):
    return pl.pallas_call(
        local_kernel,
        out_shape=[
            jax.ShapeDtypeStruct((CHIP, HALF), BF16),
            jax.ShapeDtypeStruct((CHIP, HALF), F32),
        ],
        in_specs=[VMEM] * 4,
        out_specs=[VMEM] * 2,
        compiler_params=pltpu.CompilerParams(vmem_limit_bytes=12 * 2**20),
        cost_estimate=pl.CostEstimate(
            flops=8 * CHIP * SPAN * HDIM, bytes_accessed=5 * 2**20, transcendentals=CHIP * HALF
        ),
    )(mine, other, key, value)


def finish_kernel(mine, info, query, inside, within, got_0, got_1, got_2, got_3, gain, out):
    core = info[0]
    first = core if mine else 1 - core
    for h in range(2):
        cols = slice(h * HDIM, (h + 1) * HDIM)
        gain_here = gain[:, pl.ds(pl.multiple_of(core * HALF + h * HDIM, HDIM), HDIM)]
        earlier = jnp.zeros((HDIM, HDIM), F32)
        for step, got in enumerate((got_0, got_1, got_2, got_3)):
            earlier = earlier + jnp.where(info[1 + step] > 0, got[h].astype(F32), 0.0)
        for b in range(SLAB // SPAN):
            at = pl.ds(pl.multiple_of(first * SLAB + b * SPAN, SPAN), SPAN)
            state = (earlier + within[first * (SLAB // SPAN) + b, h]).astype(BF16)
            attended = inside[at, cols] + jnp.dot(
                query[at, cols], state, preferred_element_type=F32
            )
            scale = lax.rsqrt(jnp.mean(attended * attended, axis=-1, keepdims=True) + 1e-06)
            out[b * SPAN : (b + 1) * SPAN, cols] = (attended * scale * gain_here).astype(BF16)


def finish(mine, *args):
    return pl.pallas_call(
        functools.partial(finish_kernel, mine),
        out_shape=jax.ShapeDtypeStruct((SLAB, HALF), BF16),
        in_specs=[SMEM] + [VMEM] * 8,
        out_specs=VMEM,
        compiler_params=pltpu.CompilerParams(vmem_limit_bytes=12 * 2**20),
        cost_estimate=pl.CostEstimate(
            flops=4 * SLAB * HDIM * HDIM, bytes_accessed=2 * 2**20, transcendentals=0
        ),
    )(*args)


def after(value, *others):
    return lax.optimization_barrier((value, others))[0]


def pace_kernel(piece, out):
    pass


def pace(piece):
    return pl.pallas_call(
        pace_kernel,
        out_shape=jax.ShapeDtypeStruct(piece.shape, piece.dtype),
        in_specs=[ANY],
        out_specs=ANY,
        input_output_aliases={0: 0},
        compiler_params=pltpu.CompilerParams(vmem_limit_bytes=2**20),
        cost_estimate=pl.CostEstimate(flops=2500000000, bytes_accessed=0, transcendentals=0),
    )(piece)


def gather(tokens, weights, core):
    even = jnp.concatenate([tokens[:, :ROWS], tokens[:, 2 * ROWS : 3 * ROWS]], axis=1)
    odd = jnp.concatenate([tokens[:, ROWS : 2 * ROWS], tokens[:, 3 * ROWS :]], axis=1)
    own = jnp.where(core == 0, even, odd)
    theirs = lax.ppermute(jnp.where(core == 0, odd, even), "seq", SWAP)
    rings = [[own], [theirs]]
    for _ in range(1, Z):
        for j, ring in enumerate(rings):
            ring.append(pace(lax.ppermute(ring[-1], ("seq", "head"), ring_pairs(j))))
    first, second = rings
    streams = list(weights)
    for step in range(3):
        got = [lax.ppermute(streams[j], "seq", cube_pairs(j, step)) for j in range(2)]
        pairs = list(zip(streams, got))
        if step < 2:
            streams = [jnp.concatenate(pair, axis=0) for pair in pairs]
    blocks = []
    for low, high in ((0, 2 * HALF), (2 * HALF, 3 * HALF)):
        near = [jnp.concatenate([part[:, low:high] for part in pair], axis=0) for pair in pairs]
        if low:
            near = [after(part, first[-1]) for part in near]
        blocks.append([[near[j], lax.ppermute(near[j], "seq", cube_pairs(j, 3))] for j in range(2)])
    pieces = zip(first, second[:1] + second[:0:-1])
    return [p for pair in pieces for p in pair], blocks


def local(tokens, w_query, w_key, w_value, gain):
    index = (lax.axis_index("seq") * Z + lax.axis_index("head")).astype(jnp.uint32)
    core = (lax.axis_index("seq").astype(jnp.uint32)) % C
    tokens, index, core = lax.optimization_barrier((tokens, index, core))
    table = jnp.asarray(place_table())
    info = lax.dynamic_slice(table, (index, jnp.uint32(0)), (1, table.shape[1]))[0]
    low, high = (
        jnp.concatenate([w[:, j * HALF : (j + 1) * HALF] for w in (w_key, w_value, w_query)], axis=1)
        for j in range(2)
    )
    halves = [jnp.where(core == 0, high, low), jnp.where(core == 0, low, high)]
    pieces, (kv_blocks, q_blocks) = gather(tokens, halves, core)

    kv_theirs = product(after(info, kv_blocks[1][1]), pieces, kv_blocks, 0)
    kv_got = lax.ppermute(kv_theirs, "seq", SWAP)
    kv_mine = product(info, pieces, kv_blocks, 1)
    key, value, within, total = pair_states(kv_mine, kv_got)

    q_theirs = product(after(info, total), pieces, q_blocks, 0)
    q_got = lax.ppermute(q_theirs, "seq", SWAP)
    q_mine = product(after(info, total), pieces, q_blocks, 1)
    got, group = [], total
    for step, dim in enumerate((0, 2, 1, 3)):
        if got:
            group = (group.astype(F32) + got[-1].astype(F32)).astype(BF16)
        if step == 2:
            group = after(group, q_theirs)
        if step == 3:
            group = after(group, q_mine)
        got.append(lax.ppermute(group, "seq", exchange_pairs(dim)))
    query, inside = local_part(q_mine, q_got, key, value)

    last = (info, query, inside, within, *got, gain.reshape(1, 2 * HALF))
    out_got = lax.ppermute(finish(False, *last), "seq", SWAP)
    out_mine = finish(True, *last)
    return jnp.concatenate(
        [jnp.where(core == 0, out_mine, out_got), jnp.where(core == 0, out_got, out_mine)], axis=1
    )


def solution(mesh):
    in_specs = (P("seq", "head"), P("seq", "head"), P("seq", "head"), P("seq", "head"), P("head"))
    out_specs = P("seq", "head")
    return jax.shard_map(local, mesh=mesh, in_specs=in_specs, out_specs=out_specs, check_vma=False)
```

```python
import functools

import jax
import jax.numpy as jnp
import numpy as np
from jax import lax
from jax.experimental import pallas as pl
from jax.experimental.pallas import tpu as pltpu
from jax.sharding import PartitionSpec as P

HDIM = 128
SPAN = 256
Y, X, C, Z = 4, 4, 2, 8
ROWS = 192
PIECE = 2 * ROWS
SLAB = 512
CHIP = C * SLAB
HALF = 256
PLACES = 5
BLOCKS = 2
F32, BF16 = jnp.float32, jnp.bfloat16
DIMS = (
    lambda y, x: (y, x ^ 1),
    lambda y, x: (y ^ 1, x),
    lambda y, x: (y, x ^ 3),
    lambda y, x: (y ^ 3, x),
)
ANY = pl.BlockSpec(memory_space=pl.ANY)
VMEM = pl.BlockSpec(memory_space=pltpu.VMEM)
SMEM = pl.BlockSpec(memory_space=pltpu.SMEM)


def seq_of(y, x, c):
    return (y * X + x) * C + c


def chips():
    return [(y, x) for y in range(Y) for x in range(X)]


def dim_of(stream, core, step):
    return (2 * stream + core + step) % 4


def cube_pairs(stream, step):
    return [
        (seq_of(y, x, c), seq_of(*DIMS[dim_of(stream, c, step)](y, x), c))
        for y, x in chips()
        for c in range(C)
    ]


def ring_pairs():
    return [
        (s * Z + z, s * Z + (z + (1 if s % C == 0 else -1)) % Z)
        for s in range(Y * X * C)
        for z in range(Z)
    ]


SWAP = [(s, s ^ 1) for s in range(Y * X * C)]


def exchange_pairs(dim):
    return [(seq_of(y, x, c), seq_of(*DIMS[dim](y, x), c)) for y, x in chips() for c in range(C)]


def place_table():
    table = np.zeros((Y * X * C, Z, PLACES + 4 * Z), np.int32)
    for y, x in chips():
        for c in range(C):
            for z in range(Z):
                places = []
                for stream in range(2):
                    for k in range(Z):
                        for e in range(2):
                            source = 2 * ((z - k if c == 0 else z + k) % Z) + e
                            dx, dy = (source % X) ^ x, (source // X) ^ y
                            bits = (
                                (dx & 1) ^ (dx >> 1),
                                (dy & 1) ^ (dy >> 1),
                                dx >> 1,
                                dy >> 1,
                            )
                            places.append(
                                sum(bits[dim_of(stream, c, step)] << step for step in range(4))
                            )
                after_partner = [x & 1, x >> 1, y & 1, y >> 1]
                table[seq_of(y, x, c), z] = [c] + after_partner + places
    return table.reshape(Y * X * C * Z, PLACES + 4 * Z)


def silu(u):
    return u / (1.0 + jnp.exp(-u))


def product_kernel(mine, info, *refs):
    tokens, weights, (out, piled) = refs[: 2 * Z], refs[2 * Z : 2 * Z + BLOCKS], refs[-2:]
    core = info[0]
    for slab in range(2):
        first = pl.multiple_of(SLAB * (core if slab == 0 else 1 - core), SLAB)
        total = None
        for k in range(0, Z, 2):
            deep = slice(k * PIECE, (k + 2) * PIECE)
            if slab == 0:
                for at in range(2 * k, 2 * k + 4):
                    place = info[PLACES + mine * 2 * Z + at]
                    row = pl.ds(pl.multiple_of((place % 8) * ROWS, ROWS), ROWS)
                    one, two = (w[row, :] for w in weights)
                    piled[at * ROWS : (at + 1) * ROWS] = jnp.where(place < 8, one, two)
            piece = jnp.concatenate(
                [tokens[2 * k + slab][...], tokens[2 * k + 2 + slab][...]], axis=1
            )
            some = jnp.dot(piece, piled[deep], preferred_element_type=F32)
            total = some if total is None else total + some
        out[pl.ds(first, SLAB), :] = total.astype(out.dtype)


def product(info, tokens, blocks, mine):
    width = blocks[mine][0].shape[1]
    return pl.pallas_call(
        functools.partial(product_kernel, mine),
        out_shape=jax.ShapeDtypeStruct((CHIP, width), F32 if mine else BF16),
        in_specs=[SMEM] + [VMEM] * (2 * Z + BLOCKS),
        out_specs=VMEM,
        scratch_shapes=[pltpu.VMEM((Z * PIECE, width), BF16)],
        compiler_params=pltpu.CompilerParams(vmem_limit_bytes=20 * 2**20),
        cost_estimate=pl.CostEstimate(
            flops=2 * CHIP * Z * PIECE * width, bytes_accessed=2**20, transcendentals=0
        ),
    )(info, *tokens, *blocks[mine])


def pairs_kernel(mine, other, key, value, within, total):
    for h in range(2):
        running = jnp.zeros((HDIM, HDIM), F32)
        for b in range(CHIP // SPAN):
            rows = slice(b * SPAN, (b + 1) * SPAN)
            got = []
            for at, out in ((0, key), (HALF, value)):
                cols = slice(at + h * HDIM, at + (h + 1) * HDIM)
                u = mine[rows, cols] + other[rows, cols].astype(F32)
                got.append(silu(u).astype(BF16))
                out[rows, h * HDIM : (h + 1) * HDIM] = got[-1]
            within[b, h] = running
            running = running + lax.dot_general(
                *got, (((0,), (0,)), ((), ())), preferred_element_type=F32
            )
        total[h] = running.astype(BF16)


def pair_states(mine, other):
    return pl.pallas_call(
        pairs_kernel,
        out_shape=[
            jax.ShapeDtypeStruct((CHIP, HALF), BF16),
            jax.ShapeDtypeStruct((CHIP, HALF), BF16),
            jax.ShapeDtypeStruct((CHIP // SPAN, 2, HDIM, HDIM), F32),
            jax.ShapeDtypeStruct((2, HDIM, HDIM), BF16),
        ],
        in_specs=[VMEM] * 2,
        out_specs=[VMEM] * 4,
        compiler_params=pltpu.CompilerParams(vmem_limit_bytes=12 * 2**20),
        cost_estimate=pl.CostEstimate(
            flops=2 * CHIP * 2 * HDIM * HDIM, bytes_accessed=5 * 2**20, transcendentals=CHIP * 512
        ),
    )(mine, other)


def local_kernel(mine, other, key, value, query, inside):
    causal = lax.broadcasted_iota(jnp.int32, (SPAN, SPAN), 0) >= lax.broadcasted_iota(
        jnp.int32, (SPAN, SPAN), 1
    )
    for b in range(CHIP // SPAN):
        for h in range(2):
            at = (slice(b * SPAN, (b + 1) * SPAN), slice(h * HDIM, (h + 1) * HDIM))
            q = silu(mine[at] + other[at].astype(F32)).astype(BF16)
            query[at] = q
            scores = lax.dot_general(
                q, key[at], (((1,), (1,)), ((), ())), preferred_element_type=F32
            )
            scores = jnp.where(causal, scores, 0.0).astype(BF16)
            inside[at] = jnp.dot(scores, value[at], preferred_element_type=F32)


def local_part(mine, other, key, value):
    return pl.pallas_call(
        local_kernel,
        out_shape=[
            jax.ShapeDtypeStruct((CHIP, HALF), BF16),
            jax.ShapeDtypeStruct((CHIP, HALF), F32),
        ],
        in_specs=[VMEM] * 4,
        out_specs=[VMEM] * 2,
        compiler_params=pltpu.CompilerParams(vmem_limit_bytes=12 * 2**20),
        cost_estimate=pl.CostEstimate(
            flops=8 * CHIP * SPAN * HDIM, bytes_accessed=5 * 2**20, transcendentals=CHIP * HALF
        ),
    )(mine, other, key, value)


def finish_kernel(mine, info, query, inside, within, got_0, got_1, got_2, got_3, gain, out):
    core = info[0]
    first = core if mine else 1 - core
    for h in range(2):
        cols = slice(h * HDIM, (h + 1) * HDIM)
        gain_here = gain[:, pl.ds(pl.multiple_of(core * HALF + h * HDIM, HDIM), HDIM)]
        earlier = jnp.zeros((HDIM, HDIM), F32)
        for step, got in enumerate((got_0, got_1, got_2, got_3)):
            earlier = earlier + jnp.where(info[1 + step] > 0, got[h].astype(F32), 0.0)
        for b in range(SLAB // SPAN):
            at = pl.ds(pl.multiple_of(first * SLAB + b * SPAN, SPAN), SPAN)
            state = (earlier + within[first * (SLAB // SPAN) + b, h]).astype(BF16)
            attended = inside[at, cols] + jnp.dot(
                query[at, cols], state, preferred_element_type=F32
            )
            scale = lax.rsqrt(jnp.mean(attended * attended, axis=-1, keepdims=True) + 1e-06)
            out[b * SPAN : (b + 1) * SPAN, cols] = (attended * scale * gain_here).astype(BF16)


def finish(mine, *args):
    return pl.pallas_call(
        functools.partial(finish_kernel, mine),
        out_shape=jax.ShapeDtypeStruct((SLAB, HALF), BF16),
        in_specs=[SMEM] + [VMEM] * 8,
        out_specs=VMEM,
        compiler_params=pltpu.CompilerParams(vmem_limit_bytes=12 * 2**20),
        cost_estimate=pl.CostEstimate(
            flops=4 * SLAB * HDIM * HDIM, bytes_accessed=2 * 2**20, transcendentals=0
        ),
    )(*args)


def after(value, *others):
    return lax.optimization_barrier((value, others))[0]


def pace_kernel(piece, out):
    pass


def pace(piece):
    return pl.pallas_call(
        pace_kernel,
        out_shape=jax.ShapeDtypeStruct(piece.shape, piece.dtype),
        in_specs=[ANY],
        out_specs=ANY,
        input_output_aliases={0: 0},
        compiler_params=pltpu.CompilerParams(vmem_limit_bytes=2**20),
        cost_estimate=pl.CostEstimate(flops=2500000000, bytes_accessed=0, transcendentals=0),
    )(piece)


def part_kernel(core, tokens, own, other):
    even = jnp.concatenate([tokens[:, :ROWS], tokens[:, 2 * ROWS : 3 * ROWS]], axis=1)
    odd = jnp.concatenate([tokens[:, ROWS : 2 * ROWS], tokens[:, 3 * ROWS :]], axis=1)
    own[...] = jnp.where(core[0] == 0, even, odd)
    other[...] = jnp.where(core[0] == 0, odd, even)


def part_columns(core, tokens):
    return pl.pallas_call(
        part_kernel,
        out_shape=[jax.ShapeDtypeStruct((SLAB, PIECE), BF16)] * 2,
        in_specs=[SMEM, VMEM],
        out_specs=[VMEM] * 2,
        compiler_params=pltpu.CompilerParams(vmem_limit_bytes=8 * 2**20),
        cost_estimate=pl.CostEstimate(flops=2**20, bytes_accessed=2**21, transcendentals=0),
    )(core, tokens)


def last_step(near):
    return [[part, lax.ppermute(part, "seq", cube_pairs(j, 3))] for j, part in enumerate(near)]


def gather(tokens, weights, core):
    own, other = part_columns(core.astype(jnp.int32).reshape(1), tokens)
    theirs = lax.ppermute(other, "seq", SWAP)
    ring = ring_pairs()

    def pass_on(piece):
        return lax.ppermute(piece, ("seq", "head"), ring)

    first, second = [own], [theirs]
    for k in range(1, Z):
        for stream in (first, second):
            piece = stream[-1]
            stream.append(pace(pass_on(piece)))
    streams = list(weights)
    for step in range(3):
        got = [lax.ppermute(streams[j], "seq", cube_pairs(j, step)) for j in range(2)]
        pairs = list(zip(streams, got))
        if step < 2:
            streams = [jnp.concatenate(pair, axis=0) for pair in pairs]
    near_kv, near_q = (
        [jnp.concatenate([part[:, cut] for part in pair], axis=0) for pair in pairs]
        for cut in (slice(0, 2 * HALF), slice(2 * HALF, 3 * HALF))
    )
    blocks = last_step(near_kv)
    pieces = zip(first, second)
    return [p for pair in pieces for p in pair], blocks, near_q


def local(tokens, w_query, w_key, w_value, gain):
    index = (lax.axis_index("seq") * Z + lax.axis_index("head")).astype(jnp.uint32)
    core = (lax.axis_index("seq").astype(jnp.uint32)) % C
    tokens, index, core = lax.optimization_barrier((tokens, index, core))
    table = jnp.asarray(place_table())
    info = lax.dynamic_slice(table, (index, jnp.uint32(0)), (1, table.shape[1]))[0]
    low, high = (
        jnp.concatenate([w[:, j * HALF : (j + 1) * HALF] for w in (w_key, w_value, w_query)], axis=1)
        for j in range(2)
    )
    halves = [jnp.where(core == 0, high, low), jnp.where(core == 0, low, high)]
    pieces, kv_blocks, near_q = gather(tokens, halves, core)

    kv_theirs = product(after(info, kv_blocks[1][1]), pieces, kv_blocks, 0)
    kv_got = lax.ppermute(kv_theirs, "seq", SWAP)
    kv_mine = product(info, pieces, kv_blocks, 1)
    key, value, within, total = pair_states(kv_mine, kv_got)

    q_blocks = last_step([after(part, total) for part in near_q])
    got, group = [], total
    for step, dim in enumerate((0, 2, 1, 3)):
        if got:
            group = (group.astype(F32) + got[-1].astype(F32)).astype(BF16)
        if step == 3:
            q_theirs = product(after(info, got[2]), pieces, q_blocks, 0)
        got.append(lax.ppermute(group, "seq", exchange_pairs(dim)))
    q_got = lax.ppermute(q_theirs, "seq", SWAP)
    q_mine = product(after(info, got[2]), pieces, q_blocks, 1)
    query, inside = local_part(q_mine, q_got, key, value)

    last = (info, query, inside, within, *got, gain.reshape(1, 2 * HALF))
    out_got = lax.ppermute(finish(False, *last), "seq", SWAP)
    out_mine = finish(True, *last)
    return jnp.concatenate(
        [jnp.where(core == 0, out_mine, out_got), jnp.where(core == 0, out_got, out_mine)], axis=1
    )


def solution(mesh):
    in_specs = (P("seq", "head"), P("seq", "head"), P("seq", "head"), P("seq", "head"), P("head"))
    out_specs = P("seq", "head")
    return jax.shard_map(local, mesh=mesh, in_specs=in_specs, out_specs=out_specs, check_vma=False)
```
